32 devices in a mesh: members: 2 (over x), lon: 16 (over z, y, core).
Axes of the slice: x: 2, y: 2, z: 4, core: 2. Of those that a mesh axis runs over, the one named last changes fastest.
Arguments:
- analysis_grad: bfloat16 [32768, 450], P(('members', 'lon')), parts along dimension 0, may hold values from -6 to 6
- requests: int32 [48, 256], P('lon'), may hold values from 0 to 1023
- slot_pos: int32 [32768, 16], P('lon'), may hold values from 0 to 767
- slot_weight: float32 [32768, 16], P('lon'), may hold values from 0.05 to 1
- slot_count: int32 [32768], P('lon'), may hold values from 1 to 16
- fold_src: int32 [1024], P('lon'), may hold values from 0 to 63
Outputs:
- ocean_grad: bfloat16 [65536, 450], P(('members', 'lon')), parts along dimension 0
The draws below stay inside these ranges and needn't reach their ends.
There are 2 independent parts, one for each index of `members`. The reference program is written for one: setup_inputs(seed, part) draws one part's arguments, and reference() takes and returns one part's arrays. A program takes and returns all parts, laid end to end along the dimension named above; an argument that names none is the same for every part. Nothing has to cross between parts.
Inputs may be any that keep to these rules, and one draw needn't show every extreme that they name: `requests`: local row numbers within the owner's block of 1024 analysis cells.
All inputs are finite; a program needn't handle non-finite values.
Results may differ from the reference program's by a relative error of at most 0.0041.
Values may be sent and summed in bfloat16 or wider, within the bound.
No kernel may reach another device: no remote copies, remote signals or barrier semaphores. Data moves between devices by JAX's collectives and lax.ppermute only.
A program may use at most 64 MiB of HBM per device.

```python
import math
import jax
import jax.numpy as jnp
import numpy as np
from jax import lax

K = 16
NEAR = 3
A_DEV = 1024
O_DEV = 2048
CAP = 256
FOLD = 64
COLS = 450
A_TOTAL = 16384
O_TOTAL = 32768
ASKS = 48
FOLDS = 1024
N_LON = 16


def touch_ends(array, stream_key, low, largest):
    dims = array.shape
    index_at = [jax.random.randint(jax.random.fold_in(stream_key, axis), (), 0, dims[axis]) for axis in range(len(dims))]
    array = array.at[tuple(index_at)].set(low)
    longest = dims.index(max(dims))
    index_at[longest] = (index_at[longest] + 1) % dims[longest]
    return array.at[tuple(index_at)].set(largest)


def level_of(rng, dims, shards, low, top_value):
    factor_of = 1.0
    for axis_at, shards_of in shards:
        steps = jax.random.uniform(jax.random.fold_in(jax.random.fold_in(rng, 6), axis_at), (shards_of,), jnp.float32, low / len(shards), top_value / len(shards))
        factor_of = factor_of * jnp.repeat(jnp.exp(steps), dims[axis_at] // shards_of).reshape((-1,) + (1,) * (len(dims) - 1 - axis_at))
    return factor_of


def cumulative_ranks(amount, lean):
    portions = [(1 << 20) // math.isqrt(grade ** lean) + 1 for grade in range(1, amount + 1)]
    deviation = 1 + sum(portions) // (1 << 30)
    return np.cumsum(np.array([max(1, weight // deviation) for weight in portions]))


def ranked_ids(own_key, extent, count, lean):
    grid = cumulative_ranks(count, lean)
    pick = jax.random.randint(jax.random.fold_in(own_key, 1), extent, 0, int(grid[count - 1]))
    grade = jnp.searchsorted(jnp.asarray(grid, jnp.int32), pick, side="right")
    return jax.random.permutation(jax.random.fold_in(own_key, 2), count)[grade].astype(jnp.int32)


def centred(own_key, extent, deviation, bound, cuts=(), kind=jnp.bfloat16):
    level = level_of(own_key, extent, cuts, -0.22, 0.18) if cuts else 1.0
    result = jax.random.normal(own_key, extent, jnp.float32) * deviation * level
    return jnp.minimum(jnp.maximum(result, -bound), bound).astype(kind)


def setup_inputs(seed: int = 0, part: int = 0) -> dict:
    key_list = jax.random.split(jax.random.key(seed), 7)
    part_keys = jax.random.split(jax.random.fold_in(key_list[6], part), 7)
    analysis_grad = centred(part_keys[0], (A_TOTAL, COLS), 1.0, 6.0, ((0, 16),))
    requests = touch_ends(jax.random.randint(key_list[1], (ASKS, CAP), 0, A_DEV), jax.random.fold_in(key_list[1], 1), 0, A_DEV - 1).astype(jnp.int32)
    slot_pos = touch_ends(ranked_ids(key_list[2], (O_TOTAL, K), NEAR * CAP, 1), jax.random.fold_in(key_list[2], 3), 0, (NEAR * CAP) - 1).astype(jnp.int32)
    slot_weight = jnp.clip(jnp.exp(math.log(1.0) - 2.9957323 * jax.random.uniform(key_list[3], (O_TOTAL, K), jnp.float32) ** level_of(key_list[3], (O_TOTAL, K), ((0, 16),), -0.2, 0.2)), 0.05, 1.0)
    slot_count = touch_ends(jax.random.randint(key_list[4], (O_TOTAL,), 1, K + 1), jax.random.fold_in(key_list[4], 1), 1, K).astype(jnp.int32)
    fold_src = touch_ends(jax.random.randint(key_list[5], (FOLDS,), 0, FOLD), jax.random.fold_in(key_list[5], 1), 0, FOLD - 1).astype(jnp.int32)
    return {"analysis_grad": analysis_grad, "requests": requests, "slot_pos": slot_pos, "slot_weight": slot_weight, "slot_count": slot_count, "fold_src": fold_src}


def normalized(slot_weight, slot_count):
    valid = jnp.arange(K, dtype=jnp.int32)[None, :] < slot_count[:, None]
    masked = jnp.where(valid, slot_weight, jnp.float32(0.0))
    return masked / jnp.sum(masked, axis=1, keepdims=True)


def pull_block(block, analysis_grad, requests, slot_pos, norm_f):
    asked = lax.dynamic_slice_in_dim(requests, (block * NEAR).astype(jnp.int32), NEAR, 0)
    owners = ((block + jnp.arange(NEAR, dtype=jnp.int32) - 1) % N_LON).astype(jnp.int32)
    fetched = analysis_grad[(owners[:, None] * A_DEV + asked).reshape(-1)]
    start = (block * O_DEV).astype(jnp.int32)
    places = lax.dynamic_slice_in_dim(slot_pos, start, O_DEV, 0)
    weights = lax.dynamic_slice_in_dim(norm_f, start, O_DEV, 0)
    taken = fetched[places].astype(jnp.float32)
    return jnp.einsum("ok,okc->oc", weights, taken, precision=lax.Precision.HIGHEST)


def reference(analysis_grad, requests, slot_pos, slot_weight, slot_count, fold_src):
    norm_w = normalized(slot_weight, slot_count)
    norm_b = lax.optimization_barrier(norm_w.astype(jnp.bfloat16))
    norm_f = norm_b.astype(jnp.float32)
    blocks = jnp.arange(N_LON, dtype=jnp.int32)
    pulled = lax.map(lambda b: pull_block(b, analysis_grad, requests, slot_pos, norm_f), blocks)
    flat = pulled.reshape(N_LON * O_DEV, COLS)
    partner = ((blocks + N_LON // 2) % N_LON).astype(jnp.int32)
    mirror = partner[:, None] * O_DEV + (O_DEV - FOLD) + fold_src.reshape(N_LON, FOLD)
    folded = pulled[:, O_DEV - FOLD:, :] + flat[mirror.reshape(-1)].reshape(N_LON, FOLD, COLS)
    whole = jnp.concatenate([pulled[:, :O_DEV - FOLD, :], folded], axis=1)
    return whole.reshape(N_LON * O_DEV, COLS).astype(jnp.bfloat16)
```

```python
import functools

import jax
import jax.numpy as jnp
from jax import lax
from jax.experimental import pallas as pl
from jax.experimental.pallas import tpu as pltpu
from jax.sharding import PartitionSpec as P

LANES = 128
PACK = 16
VMEM = pl.BlockSpec(memory_space=pltpu.VMEM)


def passed_along(block, axis, distance):
    count = lax.axis_size(axis)
    route = [((i - distance) % count, i) for i in range(count)]
    return lax.ppermute(block, axis, route)


def row_ids(shape):
    return lax.broadcasted_iota(jnp.int32, shape, 0)


def weights_kernel(pos_ref, weight_ref, count_ref, w_ref, *, near, cap):
    slots, cells = pos_ref.shape

    def one_tile(tile, carry):
        lanes = pl.ds(pl.multiple_of(tile * LANES, LANES), LANES)
        pos = pos_ref[:, lanes]
        valid = row_ids((slots, LANES)) < count_ref[:, lanes]
        masked = jnp.where(valid, weight_ref[:, lanes], jnp.float32(0.0))
        scale = masked / jnp.sum(masked, axis=0, keepdims=True)
        scale = scale.astype(jnp.bfloat16).astype(jnp.float32)
        merged = jnp.zeros((slots, LANES), jnp.float32)
        for k in range(slots):
            merged += jnp.where(pos == pos[k : k + 1], scale[k : k + 1], jnp.float32(0.0))
        spread = [jnp.broadcast_to(merged[k : k + 1], (PACK, LANES)).astype(jnp.bfloat16) for k in range(slots)]
        row = row_ids((PACK, LANES)).astype(jnp.float32).astype(jnp.bfloat16)
        for piece in range(near):
            local = pos - piece * cap
            local = jnp.where((local >= 0) & (local < cap), local, -1).astype(jnp.float32)
            place = [jnp.broadcast_to(local[k : k + 1], (PACK, LANES)).astype(jnp.bfloat16) for k in range(slots)]
            for group in range(cap // PACK):
                here = row + jnp.bfloat16(group * PACK)
                acc = jnp.zeros((PACK, LANES), jnp.bfloat16)
                for k in range(slots):
                    acc = jnp.where(place[k] == here, spread[k], acc)
                w_ref[pl.ds(piece * cap + group * PACK, PACK), lanes] = acc
        return carry

    lax.fori_loop(0, cells // LANES, one_tile, 0)


def dense_weights(pos, weight, count, near, cap):
    slots, cells = pos.shape
    return pl.pallas_call(
        functools.partial(weights_kernel, near=near, cap=cap),
        out_shape=jax.ShapeDtypeStruct((near * cap, cells), jnp.bfloat16),
        in_specs=[VMEM] * 3,
        out_specs=VMEM,
        compiler_params=pltpu.CompilerParams(vmem_limit_bytes=16 * 2**20),
        cost_estimate=pl.CostEstimate(flops=near * cap * cells * slots * 2, bytes_accessed=near * cap * cells * 2, transcendentals=0),
    )(pos, weight, count)


def chosen(grad, wanted):
    hit = row_ids((grad.shape[1], wanted.shape[1])) == wanted
    onehot = jnp.where(hit, jnp.float32(1.0), jnp.float32(0.0)).astype(jnp.bfloat16)
    return jnp.dot(grad, onehot, preferred_element_type=jnp.float32).astype(jnp.bfloat16)


def pick_kernel(grad_ref, own_ref, west_ref, east_ref, own_out, west_out, east_out):
    grad = grad_ref[...]
    own_out[...] = chosen(grad, own_ref[1:2, :])
    west_out[...] = chosen(grad, west_ref[2:3, :])
    east_out[...] = chosen(grad, east_ref[0:1, :])


def picked(grad, own, west, east):
    cols, cap = grad.shape[0], own.shape[1]
    shape = jax.ShapeDtypeStruct((cols, cap), jnp.bfloat16)
    return pl.pallas_call(
        pick_kernel,
        out_shape=(shape,) * 3,
        in_specs=[VMEM] * 4,
        out_specs=(VMEM,) * 3,
        compiler_params=pltpu.CompilerParams(vmem_limit_bytes=16 * 2**20),
    )(grad, own, west, east)


def mixed(parts, w_ref, lanes):
    cap = parts[0].shape[1]
    acc = None
    for i, part in enumerate(parts):
        term = jnp.dot(part[...], w_ref[pl.ds(i * cap, cap), lanes], preferred_element_type=jnp.float32)
        acc = term if acc is None else acc + term
    return acc


def edge_kernel(west_ref, own_ref, east_ref, w_ref, sum_ref, edge_ref):
    cells = w_ref.shape[1]
    total = mixed((west_ref, own_ref, east_ref), w_ref, pl.ds(cells - LANES, LANES))
    sum_ref[...] = total
    edge_ref[...] = total.astype(jnp.bfloat16)


def edge_sums(west, own, east, dense):
    cols = own.shape[0]
    return pl.pallas_call(
        edge_kernel,
        out_shape=(jax.ShapeDtypeStruct((cols, LANES), jnp.float32), jax.ShapeDtypeStruct((cols, LANES), jnp.bfloat16)),
        in_specs=[VMEM] * 4,
        out_specs=(VMEM,) * 2,
        compiler_params=pltpu.CompilerParams(vmem_limit_bytes=16 * 2**20),
    )(west, own, east, dense)


def body_kernel(west_ref, own_ref, east_ref, w_ref, out_ref):
    width = out_ref.shape[1]
    lanes = pl.ds(pl.multiple_of(pl.program_id(0) * width, width), width)
    out_ref[...] = mixed((west_ref, own_ref, east_ref), w_ref, lanes).astype(jnp.bfloat16)


def body_sums(west, own, east, dense):
    cols, cells = own.shape[0], dense.shape[1]
    width = 2 * LANES
    return pl.pallas_call(
        body_kernel,
        grid=(cells // width,),
        out_shape=jax.ShapeDtypeStruct((cols, cells), jnp.bfloat16),
        in_specs=[VMEM] * 4,
        out_specs=pl.BlockSpec((cols, width), lambda i: (0, i)),
        compiler_params=pltpu.CompilerParams(vmem_limit_bytes=16 * 2**20),
        cost_estimate=pl.CostEstimate(flops=2 * cols * dense.shape[0] * cells, bytes_accessed=cols * cells * 2, transcendentals=0),
    )(west, own, east, dense)


def fold_kernel(whole_ref, sum_ref, mirror_ref, src_ref, out_ref):
    del whole_ref
    fold = src_ref.shape[1]
    first = LANES - fold
    source = jnp.concatenate([jnp.full((1, first), -1, jnp.int32), src_ref[...] + first], axis=1)
    hit = row_ids((LANES, LANES)) == source
    onehot = jnp.where(hit, jnp.float32(1.0), jnp.float32(0.0)).astype(jnp.bfloat16)
    other = jnp.dot(mirror_ref[...], onehot, preferred_element_type=jnp.float32)
    out_ref[...] = (sum_ref[...] + other).astype(jnp.bfloat16)


def folded(whole, sums, mirror, fold_src):
    cols, cells = whole.shape
    last = cells // LANES - 1
    return pl.pallas_call(
        fold_kernel,
        grid=(1,),
        out_shape=jax.ShapeDtypeStruct((cols, cells), jnp.bfloat16),
        in_specs=[pl.BlockSpec(memory_space=pl.ANY), VMEM, VMEM, VMEM],
        out_specs=pl.BlockSpec((cols, LANES), lambda i: (0, last)),
        input_output_aliases={0: 0},
        compiler_params=pltpu.CompilerParams(vmem_limit_bytes=8 * 2**20),
    )(whole, sums, mirror, fold_src)


def local(analysis_grad, requests, slot_pos, slot_weight, slot_count, fold_src):
    near, cap = requests.shape
    around = lax.axis_size("lon")
    to_west = passed_along(requests, "lon", -1)
    to_east = passed_along(requests, "lon", 1)
    dense = dense_weights(slot_pos.T, slot_weight.T, slot_count[None, :], near, cap)
    own, for_west, for_east = picked(analysis_grad.T, requests, to_east, to_west)
    from_east = passed_along(for_west, "lon", -1)
    from_west = passed_along(for_east, "lon", 1)
    sums, edge = edge_sums(from_west, own, from_east, dense)
    mirror = passed_along(edge, "lon", around // 2)
    whole = body_sums(from_west, own, from_east, dense)
    return folded(whole, sums, mirror, fold_src[None, :]).T


def solution(mesh):
    in_specs = (
        P(("members", "lon"), None),
        P("lon", None),
        P("lon", None),
        P("lon", None),
        P("lon"),
        P("lon"),
    )
    out_specs = P(("members", "lon"), None)
    return jax.shard_map(local, mesh=mesh, in_specs=in_specs, out_specs=out_specs, check_vma=False)
```

```python
import functools

import jax
import jax.numpy as jnp
from jax import lax
from jax.experimental import pallas as pl
from jax.experimental.pallas import tpu as pltpu
from jax.sharding import PartitionSpec as P

LANES = 128
PACK = 16
EARLY_TILES = 4
MIB = 2**20
VMEM = pl.BlockSpec(memory_space=pltpu.VMEM)
HBM = pl.BlockSpec(memory_space=pltpu.HBM)


def even_place():
    return lax.rem(lax.axis_index("lon"), 2) == 0


def row_ids(shape):
    return lax.broadcasted_iota(jnp.int32, shape, 0)


def lane_ids(shape):
    return lax.broadcasted_iota(jnp.int32, shape, 1)


def inner_swap(block):
    count = lax.axis_size("lon")
    return lax.ppermute(block, "lon", [(i, i ^ 1) for i in range(count)])


def outer_swap(block):
    count = lax.axis_size("lon")
    return lax.ppermute(block, "lon", [(i, (i - 1) % count if i % 2 == 0 else (i + 1) % count) for i in range(count)])


def half_away(block):
    count = lax.axis_size("lon")
    return lax.ppermute(block, "lon", [(i, (i + count // 2) % count) for i in range(count)])


def in_hbm(block):
    return pltpu.with_memory_space_constraint(block, pltpu.HBM)


def fill_tiles(pos_ref, weight_ref, count_ref, w_ref, first, tiles, near, cap):
    slots = pos_ref.shape[0]
    flip = jnp.where(even_place(), 0, near - 1)

    def one_tile(tile, carry):
        taken = pl.ds(pl.multiple_of((first + tile) * LANES, LANES), LANES)
        given = pl.ds(pl.multiple_of(tile * LANES, LANES), LANES)
        pos = pos_ref[:, taken]
        valid = row_ids((slots, LANES)) < count_ref[:, taken]
        masked = jnp.where(valid, weight_ref[:, taken], jnp.float32(0.0))
        scale = masked / jnp.sum(masked, axis=0, keepdims=True)
        scale = scale.astype(jnp.bfloat16).astype(jnp.float32)
        merged = jnp.zeros((slots, LANES), jnp.float32)
        for k in range(slots):
            merged += jnp.where(pos == pos[k : k + 1], scale[k : k + 1], jnp.float32(0.0))
        spread = [jnp.broadcast_to(merged[k : k + 1], (PACK, LANES)).astype(jnp.bfloat16) for k in range(slots)]
        row = row_ids((PACK, LANES)).astype(jnp.float32).astype(jnp.bfloat16)
        for piece in range(near):
            source = jnp.where(flip == 0, piece, near - 1 - piece)
            local = pos - source * cap
            local = jnp.where((local >= 0) & (local < cap), local, -1).astype(jnp.float32)
            place = [jnp.broadcast_to(local[k : k + 1], (PACK, LANES)).astype(jnp.bfloat16) for k in range(slots)]
            for group in range(cap // PACK):
                here = row + jnp.bfloat16(group * PACK)
                acc = jnp.zeros((PACK, LANES), jnp.bfloat16)
                for k in range(slots):
                    acc = jnp.where(place[k] == here, spread[k], acc)
                w_ref[pl.ds(piece * cap + group * PACK, PACK), given] = acc
        return carry

    lax.fori_loop(0, tiles, one_tile, 0)


def early_kernel(grad_hbm, pos_hbm, weight_hbm, count_hbm, own_hbm, grad_ref, pos_ref, weight_ref, count_ref, own_ref, w_ref, sems, *, near, cap):
    pairs = ((pos_hbm, pos_ref), (weight_hbm, weight_ref), (count_hbm, count_ref), (own_hbm, own_ref), (grad_hbm, grad_ref))
    copies = [pltpu.make_async_copy(source, target, sems.at[i]) for i, (source, target) in enumerate(pairs)]
    for copy in copies:
        copy.start()
    for copy in copies[:3]:
        copy.wait()
    tiles = w_ref.shape[1] // LANES
    fill_tiles(pos_ref, weight_ref, count_ref, w_ref, pos_ref.shape[1] // LANES - tiles, tiles, near, cap)
    for copy in copies[3:]:
        copy.wait()


def early(grad, pos, weight, count, own, tiles):
    near, cap = own.shape
    held = [jax.ShapeDtypeStruct(x.shape, x.dtype) for x in (grad, pos, weight, count, own)]
    return pl.pallas_call(
        functools.partial(early_kernel, near=near, cap=cap),
        out_shape=(*held, jax.ShapeDtypeStruct((near * cap, tiles * LANES), jnp.bfloat16)),
        in_specs=[HBM] * 5,
        out_specs=(VMEM,) * 6,
        scratch_shapes=[pltpu.SemaphoreType.DMA((5,))],
        compiler_params=pltpu.CompilerParams(vmem_limit_bytes=16 * MIB),
    )(grad, pos, weight, count, own)


def late_kernel(pos_ref, weight_ref, count_ref, w_ref, *, near, cap):
    fill_tiles(pos_ref, weight_ref, count_ref, w_ref, 0, w_ref.shape[1] // LANES, near, cap)


def late(pos, weight, count, near, cap, tiles):
    cells, slots = tiles * LANES, pos.shape[0]
    return pl.pallas_call(
        functools.partial(late_kernel, near=near, cap=cap),
        out_shape=jax.ShapeDtypeStruct((near * cap, cells), jnp.bfloat16),
        in_specs=[VMEM] * 3,
        out_specs=VMEM,
        compiler_params=pltpu.CompilerParams(vmem_limit_bytes=16 * MIB),
        cost_estimate=pl.CostEstimate(flops=near * cap * cells * slots * 2, bytes_accessed=near * cap * cells * 2, transcendentals=0),
    )(pos, weight, count)


def chosen(grad, wanted):
    hit = row_ids((grad.shape[1], wanted.shape[1])) == wanted
    onehot = jnp.where(hit, jnp.float32(1.0), jnp.float32(0.0)).astype(jnp.bfloat16)
    return jnp.dot(grad, onehot, preferred_element_type=jnp.float32).astype(jnp.bfloat16)


def outer_pick_kernel(grad_ref, asked_ref, out_ref):
    near = asked_ref.shape[0]
    wanted = jnp.where(even_place(), asked_ref[near - 1 : near, :], asked_ref[0:1, :])
    out_ref[...] = chosen(grad_ref[...], wanted)


def inner_pick_kernel(grad_ref, asked_ref, own_ref, out_ref, own_out):
    near = asked_ref.shape[0]
    wanted = jnp.where(even_place(), asked_ref[0:1, :], asked_ref[near - 1 : near, :])
    out_ref[...] = chosen(grad_ref[...], wanted)
    own_out[...] = chosen(grad_ref[...], own_ref[near // 2 : near // 2 + 1, :])


def picked(kernel, outputs, grad, *asked):
    shape = jax.ShapeDtypeStruct((grad.shape[0], asked[0].shape[1]), grad.dtype)
    return pl.pallas_call(
        kernel,
        out_shape=(shape,) * outputs,
        in_specs=[VMEM] * (1 + len(asked)),
        out_specs=(VMEM,) * outputs,
        compiler_params=pltpu.CompilerParams(vmem_limit_bytes=16 * MIB),
    )(grad, *asked)


def mixed(parts, w_ref, lanes):
    cap = parts[0].shape[1]
    acc = None
    for i, part in enumerate(parts):
        term = jnp.dot(part[...], w_ref[pl.ds(i * cap, cap), lanes], preferred_element_type=jnp.float32)
        acc = term if acc is None else acc + term
    return acc


def edge_kernel(outer_ref, own_ref, inner_ref, w_ref, sum_ref, edge_ref):
    cells, cols, half = w_ref.shape[1], own_ref.shape[0], edge_ref.shape[0]
    total = mixed((outer_ref, own_ref, inner_ref), w_ref, pl.ds(cells - LANES, LANES))
    sum_ref[pl.ds(cols // 8 * 8, 2 * half - cols // 8 * 8), :] = jnp.zeros((2 * half - cols // 8 * 8, LANES), jnp.float32)
    sum_ref[0:cols, :] = total
    upper = pltpu.roll(sum_ref[0:half, :], LANES // 2, 1)
    packed = jnp.where(lane_ids((half, LANES)) < LANES // 2, upper, sum_ref[half : 2 * half, :])
    edge_ref[...] = packed.astype(jnp.bfloat16)


def edge_sums(outer, own, inner, dense):
    cols = own.shape[0]
    half = -(-cols // (2 * PACK)) * PACK
    return pl.pallas_call(
        edge_kernel,
        out_shape=(jax.ShapeDtypeStruct((2 * half, LANES), jnp.float32), jax.ShapeDtypeStruct((half, LANES), jnp.bfloat16)),
        in_specs=[VMEM] * 4,
        out_specs=(VMEM,) * 2,
        compiler_params=pltpu.CompilerParams(vmem_limit_bytes=16 * MIB),
    )(outer, own, inner, dense)


def body_kernel(outer_ref, own_ref, inner_ref, late_ref, early_ref, out_hbm, buffer, sems, *, steps):
    for i, (start, width) in enumerate(steps):
        ahead = late_ref.shape[1]
        w_ref, inside = (late_ref, start) if start < ahead else (early_ref, start - ahead)
        buffer[:, pl.ds(start, width)] = mixed((outer_ref, own_ref, inner_ref), w_ref, pl.ds(inside, width)).astype(jnp.bfloat16)
        pltpu.make_async_copy(buffer.at[:, pl.ds(start, width)], out_hbm.at[:, pl.ds(start, width)], sems.at[i]).start()
    for i, (start, width) in enumerate(steps):
        pltpu.make_async_copy(buffer.at[:, pl.ds(start, width)], out_hbm.at[:, pl.ds(start, width)], sems.at[i]).wait()


def cuts(first, last, width):
    return [(start, min(width, last - start)) for start in range(first, last, width)]


def body_sums(outer, own, inner, late_w, early_w):
    cols, ahead = own.shape[0], late_w.shape[1]
    cells = ahead + early_w.shape[1]
    steps = cuts(0, ahead, 4 * LANES) + cuts(ahead, cells - LANES, 4 * LANES)
    return pl.pallas_call(
        functools.partial(body_kernel, steps=steps),
        out_shape=jax.ShapeDtypeStruct((cols, cells), jnp.bfloat16),
        in_specs=[VMEM] * 5,
        out_specs=HBM,
        scratch_shapes=[pltpu.VMEM((cols, cells), jnp.bfloat16), pltpu.SemaphoreType.DMA((len(steps),))],
        compiler_params=pltpu.CompilerParams(vmem_limit_bytes=24 * MIB),
        cost_estimate=pl.CostEstimate(flops=2 * cols * late_w.shape[0] * cells, bytes_accessed=cols * cells * 2, transcendentals=0),
    )(outer, own, inner, late_w, early_w)


def fold_kernel(whole_ref, sum_ref, mirror_ref, src_ref, out_ref):
    del whole_ref
    cols, half, fold = out_ref.shape[0], mirror_ref.shape[0], src_ref.shape[1]
    unused = jnp.full((1, LANES - fold), -1, jnp.int32)
    others = []
    for shift in (0, LANES // 2):
        source = jnp.concatenate([unused, src_ref[...] + shift], axis=1)
        hit = row_ids((LANES, LANES)) == source
        onehot = jnp.where(hit, jnp.float32(1.0), jnp.float32(0.0)).astype(jnp.bfloat16)
        others.append(jnp.dot(mirror_ref[...], onehot, preferred_element_type=jnp.float32))
    other = jnp.concatenate(others, axis=0)[0:cols]
    out_ref[...] = (sum_ref[0:cols, :] + other).astype(jnp.bfloat16)


def folded(whole, sums, mirror, fold_src):
    cols, cells = whole.shape
    last = cells // LANES - 1
    return pl.pallas_call(
        fold_kernel,
        grid=(1,),
        out_shape=jax.ShapeDtypeStruct((cols, cells), jnp.bfloat16),
        in_specs=[HBM, VMEM, VMEM, VMEM],
        out_specs=pl.BlockSpec((cols, LANES), lambda i: (0, last)),
        input_output_aliases={0: 0},
        compiler_params=pltpu.CompilerParams(vmem_limit_bytes=8 * MIB),
    )(whole, sums, mirror, fold_src)


def local(analysis_grad, requests, slot_pos, slot_weight, slot_count, fold_src):
    near, cap = requests.shape
    tiles = slot_pos.shape[0] // LANES
    asked_outer = outer_swap(requests)
    asked_inner = inner_swap(requests)
    placed = [in_hbm(x) for x in (analysis_grad.T, slot_pos.T, slot_weight.T, slot_count[None, :], requests)]
    grad, pos, weight, count, own_asks, early_w = early(*placed, EARLY_TILES)
    (for_outer,) = picked(outer_pick_kernel, 1, grad, asked_outer)
    outer = outer_swap(for_outer)
    for_inner, own = picked(inner_pick_kernel, 2, grad, asked_inner, own_asks)
    inner = inner_swap(for_inner)
    late_w = late(pos, weight, count, near, cap, tiles - EARLY_TILES)
    sums, edge = edge_sums(outer, own, inner, early_w)
    mirror = half_away(edge)
    whole = body_sums(outer, own, inner, late_w, early_w)
    return folded(whole, sums, mirror, fold_src[None, :]).T


def solution(mesh):
    in_specs = (
        P(("members", "lon"), None),
        P("lon", None),
        P("lon", None),
        P("lon", None),
        P("lon"),
        P("lon"),
    )
    out_specs = P(("members", "lon"), None)
    return jax.shard_map(local, mesh=mesh, in_specs=in_specs, out_specs=out_specs, check_vma=False)
```

```python
import functools
import math

import jax
import jax.numpy as jnp
from jax import lax
from jax.experimental import pallas as pl
from jax.experimental.pallas import tpu as pltpu
from jax.sharding import PartitionSpec as P

LANES = 128
PACK = 16
MIB = 2**20
VMEM = pl.BlockSpec(memory_space=pltpu.VMEM)
HBM = pl.BlockSpec(memory_space=pltpu.HBM)


def even_place():
    return lax.rem(lax.axis_index("lon"), 2) == 0


def row_ids(shape):
    return lax.broadcasted_iota(jnp.int32, shape, 0)


def lane_ids(shape):
    return lax.broadcasted_iota(jnp.int32, shape, 1)


def outer_place(place, count):
    return (place - 1) % count if place % 2 == 0 else (place + 1) % count


def inner_swap(block):
    count = lax.axis_size("lon")
    return lax.ppermute(block, "lon", [(i, i ^ 1) for i in range(count)])


def outer_swap(block):
    count = lax.axis_size("lon")
    return lax.ppermute(block, "lon", [(i, outer_place(i, count)) for i in range(count)])


def half_away(block):
    count = lax.axis_size("lon")
    return lax.ppermute(block, "lon", [(i, (i + count // 2) % count) for i in range(count)])


def half_away_of_outer(block):
    count = lax.axis_size("lon")
    return lax.ppermute(block, "lon", [(i, (outer_place(i, count) + count // 2) % count) for i in range(count)])


def in_hbm(block):
    return pltpu.with_memory_space_constraint(block, pltpu.HBM)


def merged_weights(pos, weight, count):
    valid = row_ids(pos.shape) < count
    masked = jnp.where(valid, weight, jnp.float32(0.0))
    scale = masked / jnp.sum(masked, axis=0, keepdims=True)
    scale = scale.astype(jnp.bfloat16).astype(jnp.float32)
    merged = jnp.zeros(pos.shape, jnp.float32)
    for k in range(pos.shape[0]):
        merged += jnp.where(pos == pos[k : k + 1], scale[k : k + 1], jnp.float32(0.0))
    return merged


def spread_rows(rows, dtype):
    return [jnp.broadcast_to(rows[k : k + 1], (PACK, LANES)).astype(dtype) for k in range(rows.shape[0])]


def fill_piece(w_ref, first, lanes, count, place, spread):
    for group in range(count // PACK):
        acc = jnp.zeros((PACK, LANES), jnp.bfloat16)
        for k in range(len(place)):
            acc = jnp.where(place[k] == jnp.int16(group * PACK), spread[k], acc)
        w_ref[pl.ds(first + group * PACK, PACK), lanes] = acc


def fill_tiles(pos_ref, weight_ref, count_ref, w_ref, first, tiles, near, cap):
    even = even_place()
    row = row_ids((PACK, LANES)).astype(jnp.int16)

    def one_tile(tile, carry):
        taken = pl.ds(pl.multiple_of((first + tile) * LANES, LANES), LANES)
        given = pl.ds(pl.multiple_of(tile * LANES, LANES), LANES)
        pos = pos_ref[:, taken]
        spread = spread_rows(merged_weights(pos, weight_ref[:, taken], count_ref[:, taken]), jnp.bfloat16)
        turned = jnp.where(even, pos, pos + cap * (near - 1) - 2 * cap * lax.div(pos, cap))
        place = [x - row for x in spread_rows(turned, jnp.int16)]
        fill_piece(w_ref, 0, given, near * cap, place, spread)
        return carry

    lax.fori_loop(0, tiles, one_tile, 0, unroll=math.gcd(tiles, 3))


def ask_kernel(pos_hbm, weight_hbm, count_hbm, wanted_hbm, ask_ref, near_ref, pos_ref, weight_ref, count_ref, wanted_ref, sems):
    slots, cells = pos_hbm.shape
    near, cap = wanted_hbm.shape
    last = pl.ds(cells - LANES, LANES)
    pairs = ((pos_hbm.at[:, last], pos_ref), (weight_hbm.at[:, last], weight_ref), (count_hbm.at[:, last], count_ref), (wanted_hbm, wanted_ref))
    copies = [pltpu.make_async_copy(source, target, sems.at[i]) for i, (source, target) in enumerate(pairs)]
    for copy in copies:
        copy.start()
    for copy in copies:
        copy.wait()
    pos, even = pos_ref[...], even_place()
    local = pos - jnp.where(even, 0, (near - 1) * cap)
    local = jnp.where((local >= 0) & (local < cap), local, -1)
    wanted = jnp.where(even, wanted_ref[0:1, :], wanted_ref[near - 1 : near, :])
    for i in range(near):
        near_ref[i] = jnp.broadcast_to(wanted_ref[i : i + 1, :], (PACK, cap))
    ask_ref[0:slots, 0:LANES] = local.astype(jnp.float32)
    ask_ref[0:slots, LANES : 2 * LANES] = merged_weights(pos, weight_ref[...], count_ref[...])
    ask_ref[slots:, :] = jnp.broadcast_to(wanted, (ask_ref.shape[0] - slots, cap)).astype(jnp.float32)


def ask(pos, weight, count, wanted):
    slots, cap = pos.shape[0], wanted.shape[1]
    tile = (slots, LANES)
    return pl.pallas_call(
        ask_kernel,
        out_shape=(jax.ShapeDtypeStruct((slots + 8, cap), jnp.float32), jax.ShapeDtypeStruct((wanted.shape[0], PACK, cap), jnp.int32)),
        in_specs=[HBM] * 4,
        out_specs=(VMEM,) * 2,
        scratch_shapes=[
            pltpu.VMEM(tile, jnp.int32),
            pltpu.VMEM(tile, jnp.float32),
            pltpu.VMEM((1, LANES), jnp.int32),
            pltpu.VMEM(wanted.shape, jnp.int32),
            pltpu.SemaphoreType.DMA((4,)),
        ],
        compiler_params=pltpu.CompilerParams(vmem_limit_bytes=16 * MIB),
    )(*[in_hbm(x) for x in (pos, weight, count, wanted)])


def load_kernel(*refs):
    count = (len(refs) - 1) // 2
    copies = [pltpu.make_async_copy(refs[i], refs[count + i], refs[-1].at[i]) for i in range(count)]
    for copy in copies:
        copy.start()
    for copy in copies:
        copy.wait()


def loaded(*arrays):
    return pl.pallas_call(
        load_kernel,
        out_shape=tuple(jax.ShapeDtypeStruct(x.shape, x.dtype) for x in arrays),
        in_specs=[HBM] * len(arrays),
        out_specs=(VMEM,) * len(arrays),
        scratch_shapes=[pltpu.SemaphoreType.DMA((len(arrays),))],
        compiler_params=pltpu.CompilerParams(vmem_limit_bytes=16 * MIB),
    )(*[in_hbm(x) for x in arrays])


def late_kernel(pos_ref, weight_ref, count_ref, w_ref, *, near, cap):
    fill_tiles(pos_ref, weight_ref, count_ref, w_ref, 0, w_ref.shape[1] // LANES, near, cap)


def late(pos, weight, count, near, cap):
    slots, cells = pos.shape[0], pos.shape[1] - LANES
    return pl.pallas_call(
        functools.partial(late_kernel, near=near, cap=cap),
        out_shape=jax.ShapeDtypeStruct((near * cap, cells), jnp.bfloat16),
        in_specs=[VMEM] * 3,
        out_specs=VMEM,
        compiler_params=pltpu.CompilerParams(vmem_limit_bytes=16 * MIB),
        cost_estimate=pl.CostEstimate(flops=near * cap * cells * slots * 2, bytes_accessed=near * cap * cells * 2, transcendentals=0),
    )(pos, weight, count)


def chosen(grad, wanted):
    hit = row_ids((grad.shape[1], wanted.shape[1])) == wanted
    onehot = jnp.where(hit, jnp.float32(1.0), jnp.float32(0.0)).astype(jnp.bfloat16)
    return jnp.dot(grad, onehot, preferred_element_type=jnp.float32).astype(jnp.bfloat16)


def outer_pick_kernel(grad_ref, asked_ref, out_ref):
    rows = asked_ref.shape[0]
    out_ref[...] = chosen(grad_ref[...], asked_ref[rows - 1 : rows, :].astype(jnp.int32))


def inner_pick_kernel(grad_ref, asked_ref, own_ref, out_ref, own_out):
    near = asked_ref.shape[0]
    wanted = jnp.where(even_place(), asked_ref[0, 0:1, :], asked_ref[near - 1, 0:1, :])
    out_ref[...] = chosen(grad_ref[...], wanted)
    own_out[...] = chosen(grad_ref[...], own_ref[near // 2, 0:1, :])


def picked(kernel, outputs, grad, *asked):
    shape = jax.ShapeDtypeStruct((grad.shape[0], asked[0].shape[-1]), grad.dtype)
    return pl.pallas_call(
        kernel,
        out_shape=(shape,) * outputs,
        in_specs=[VMEM] * (1 + len(asked)),
        out_specs=(VMEM,) * outputs,
        compiler_params=pltpu.CompilerParams(vmem_limit_bytes=16 * MIB),
    )(grad, *asked)


def half_rows(cols):
    return -(-cols // (2 * PACK)) * PACK


def pack_fold(total, edge_ref, sum_ref):
    cols, half = total.shape[0], edge_ref.shape[0]
    tail = cols // 8 * 8
    sum_ref[pl.ds(tail, 2 * half - tail), :] = jnp.zeros((2 * half - tail, LANES), jnp.float32)
    sum_ref[0:cols, :] = total
    upper = pltpu.roll(sum_ref[0:half, :], LANES // 2, 1)
    packed = jnp.where(lane_ids((half, LANES)) < LANES // 2, upper, sum_ref[half : 2 * half, :])
    edge_ref[...] = packed.astype(jnp.bfloat16)


def near_fold_kernel(pos_ref, weight_ref, count_ref, own_ref, inner_ref, w_ref, edge_ref, sum_ref, *, near, cap):
    fill_tiles(pos_ref, weight_ref, count_ref, w_ref, pos_ref.shape[1] // LANES - 1, 1, near, cap)
    total = jnp.dot(own_ref[...], w_ref[cap : 2 * cap, :], preferred_element_type=jnp.float32)
    total += jnp.dot(inner_ref[...], w_ref[2 * cap : 3 * cap, :], preferred_element_type=jnp.float32)
    pack_fold(total, edge_ref, sum_ref)


def near_fold(pos, weight, count, own, inner, near):
    cols, cap = own.shape
    half = half_rows(cols)
    return pl.pallas_call(
        functools.partial(near_fold_kernel, near=near, cap=cap),
        out_shape=(jax.ShapeDtypeStruct((near * cap, LANES), jnp.bfloat16), jax.ShapeDtypeStruct((half, LANES), jnp.bfloat16)),
        in_specs=[VMEM] * 5,
        out_specs=(VMEM,) * 2,
        scratch_shapes=[pltpu.VMEM((2 * half, LANES), jnp.float32)],
        compiler_params=pltpu.CompilerParams(vmem_limit_bytes=16 * MIB),
    )(pos, weight, count, own, inner)


def far_fold_kernel(asked_ref, rows_ref, edge_ref, w_ref, sum_ref):
    slots, cap = asked_ref.shape[0] - 8, rows_ref.shape[1]
    row = row_ids((PACK, LANES)).astype(jnp.int16)
    place = [x - row for x in spread_rows(asked_ref[0:slots, 0:LANES].astype(jnp.int32), jnp.int16)]
    fill_piece(w_ref, 0, pl.ds(0, LANES), cap, place, spread_rows(asked_ref[0:slots, LANES : 2 * LANES], jnp.bfloat16))
    pack_fold(jnp.dot(rows_ref[...], w_ref[...], preferred_element_type=jnp.float32), edge_ref, sum_ref)


def far_fold(asked, rows):
    cols, cap = rows.shape
    half = half_rows(cols)
    return pl.pallas_call(
        far_fold_kernel,
        out_shape=jax.ShapeDtypeStruct((half, LANES), jnp.bfloat16),
        in_specs=[VMEM] * 2,
        out_specs=VMEM,
        scratch_shapes=[pltpu.VMEM((cap, LANES), jnp.bfloat16), pltpu.VMEM((2 * half, LANES), jnp.float32)],
        compiler_params=pltpu.CompilerParams(vmem_limit_bytes=16 * MIB),
    )(asked, rows)


def mixed(parts, w_ref, lanes):
    cap = parts[0].shape[1]
    acc = None
    for i, part in enumerate(parts):
        term = jnp.dot(part[...], w_ref[pl.ds(i * cap, cap), lanes], preferred_element_type=jnp.float32)
        acc = term if acc is None else acc + term
    return acc


def unpack_fold(mirrors, src_ref, cols):
    fold = src_ref.shape[1]
    unused = jnp.full((1, LANES - fold), -1, jnp.int32)
    halves = []
    for shift in (0, LANES // 2):
        source = jnp.concatenate([unused, src_ref[...] + shift], axis=1)
        hit = row_ids((LANES, LANES)) == source
        onehot = jnp.where(hit, jnp.float32(1.0), jnp.float32(0.0)).astype(jnp.bfloat16)
        halves.append(sum(jnp.dot(m[...], onehot, preferred_element_type=jnp.float32) for m in mirrors))
    return jnp.concatenate(halves, axis=0)[0:cols]


def body_kernel(outer_ref, own_ref, inner_ref, late_ref, last_ref, near_ref, far_ref, src_ref, out_hbm, buffer, sems, *, steps):
    parts = (outer_ref, own_ref, inner_ref)
    copies = []
    for i, (start, width) in enumerate(steps):
        lanes = pl.ds(start, width)
        if start < late_ref.shape[1]:
            total = mixed(parts, late_ref, lanes)
        else:
            total = mixed(parts, last_ref, pl.ds(0, width)) + unpack_fold((near_ref, far_ref), src_ref, own_ref.shape[0])
        buffer[:, lanes] = total.astype(jnp.bfloat16)
        copies.append(pltpu.make_async_copy(buffer.at[:, lanes], out_hbm.at[:, lanes], sems.at[i]))
        copies[-1].start()
    for copy in copies:
        copy.wait()


def body_sums(outer, own, inner, late_w, last_w, near_mirror, far_mirror, fold_src):
    cols, ahead = own.shape[0], late_w.shape[1]
    cells = ahead + LANES
    steps = [(start, min(4 * LANES, ahead - start)) for start in range(0, ahead, 4 * LANES)] + [(ahead, LANES)]
    return pl.pallas_call(
        functools.partial(body_kernel, steps=steps),
        out_shape=jax.ShapeDtypeStruct((cols, cells), jnp.bfloat16),
        in_specs=[VMEM] * 8,
        out_specs=HBM,
        scratch_shapes=[pltpu.VMEM((cols, cells), jnp.bfloat16), pltpu.SemaphoreType.DMA((len(steps),))],
        compiler_params=pltpu.CompilerParams(vmem_limit_bytes=24 * MIB),
        cost_estimate=pl.CostEstimate(flops=2 * cols * late_w.shape[0] * cells, bytes_accessed=cols * cells * 2, transcendentals=0),
    )(outer, own, inner, late_w, last_w, near_mirror, far_mirror, fold_src)


def local(analysis_grad, requests, slot_pos, slot_weight, slot_count, fold_src):
    near, cap = requests.shape
    places, raw, counts = slot_pos.T, slot_weight.T, slot_count[None, :]
    for_asking, own_asks = ask(places, raw, counts, requests)
    asked_inner = inner_swap(own_asks)
    asked_outer = outer_swap(for_asking)
    grad, pos, weight, count = loaded(analysis_grad.T, places, raw, counts)
    for_inner, own = picked(inner_pick_kernel, 2, grad, asked_inner, own_asks)
    asked_outer, for_inner = lax.optimization_barrier((asked_outer, for_inner))
    inner = inner_swap(for_inner)
    (for_outer,) = picked(outer_pick_kernel, 1, grad, asked_outer)
    outer = outer_swap(for_outer)
    last_w, near_edge = near_fold(pos, weight, count, own, inner, near)
    near_mirror = half_away(near_edge)
    far_mirror = half_away_of_outer(far_fold(asked_outer, for_outer))
    late_w = late(pos, weight, count, near, cap)
    return body_sums(outer, own, inner, late_w, last_w, near_mirror, far_mirror, fold_src[None, :]).T


def solution(mesh):
    in_specs = (
        P(("members", "lon"), None),
        P("lon", None),
        P("lon", None),
        P("lon", None),
        P("lon"),
        P("lon"),
    )
    out_specs = P(("members", "lon"), None)
    return jax.shard_map(local, mesh=mesh, in_specs=in_specs, out_specs=out_specs, check_vma=False)
```

```python
import functools
import math

import jax
import jax.numpy as jnp
from jax import lax
from jax.experimental import pallas as pl
from jax.experimental.pallas import tpu as pltpu
from jax.sharding import PartitionSpec as P

LANES = 128
PACK = 16
MIB = 2**20
FLOPS_PER_MICRO = 10**9
EARLY_TILES = 8
IPICK = 0
OPICK = 3
LOAD = 0
WA = 0
FOLD = 1
VMEM = pl.BlockSpec(memory_space=pltpu.VMEM)
HBM = pl.BlockSpec(memory_space=pltpu.HBM)


def lasting(micros):
    return pl.CostEstimate(flops=int(micros * FLOPS_PER_MICRO), bytes_accessed=0, transcendentals=0)


def even_place():
    return lax.rem(lax.axis_index("lon"), 2) == 0


def row_ids(shape):
    return lax.broadcasted_iota(jnp.int32, shape, 0)


def lane_ids(shape):
    return lax.broadcasted_iota(jnp.int32, shape, 1)


def outer_place(place, count):
    return (place - 1) % count if place % 2 == 0 else (place + 1) % count


def inner_swap(block):
    count = lax.axis_size("lon")
    return lax.ppermute(block, "lon", [(i, i ^ 1) for i in range(count)])


def outer_swap(block):
    count = lax.axis_size("lon")
    return lax.ppermute(block, "lon", [(i, outer_place(i, count)) for i in range(count)])


def half_away(block):
    count = lax.axis_size("lon")
    return lax.ppermute(block, "lon", [(i, (i + count // 2) % count) for i in range(count)])


def half_away_of_outer(block):
    count = lax.axis_size("lon")
    return lax.ppermute(block, "lon", [(i, (outer_place(i, count) + count // 2) % count) for i in range(count)])


def in_hbm(block):
    return pltpu.with_memory_space_constraint(block, pltpu.HBM)


def merged_weights(pos, weight, count):
    valid = row_ids(pos.shape) < count
    masked = jnp.where(valid, weight, jnp.float32(0.0))
    scale = masked / jnp.sum(masked, axis=0, keepdims=True)
    scale = scale.astype(jnp.bfloat16).astype(jnp.float32)
    merged = jnp.zeros(pos.shape, jnp.float32)
    for k in range(pos.shape[0]):
        merged += jnp.where(pos == pos[k : k + 1], scale[k : k + 1], jnp.float32(0.0))
    return merged


def spread_rows(rows, dtype):
    return [jnp.broadcast_to(rows[k : k + 1], (PACK, LANES)).astype(dtype) for k in range(rows.shape[0])]


def fill_piece(w_ref, first, lanes, count, place, spread):
    for group in range(count // PACK):
        acc = jnp.zeros((PACK, LANES), jnp.bfloat16)
        for k in range(len(place)):
            acc = jnp.where(place[k] == jnp.int16(group * PACK), spread[k], acc)
        w_ref[pl.ds(first + group * PACK, PACK), lanes] = acc


def fill_tiles(pos_ref, weight_ref, count_ref, w_ref, first, tiles, near, cap):
    even = even_place()
    row = row_ids((PACK, LANES)).astype(jnp.int16)

    def one_tile(tile, carry):
        taken = pl.ds(pl.multiple_of((first + tile) * LANES, LANES), LANES)
        given = pl.ds(pl.multiple_of(tile * LANES, LANES), LANES)
        pos = pos_ref[:, taken]
        spread = spread_rows(merged_weights(pos, weight_ref[:, taken], count_ref[:, taken]), jnp.bfloat16)
        turned = jnp.where(even, pos, pos + cap * (near - 1) - 2 * cap * lax.div(pos, cap))
        place = [x - row for x in spread_rows(turned, jnp.int16)]
        fill_piece(w_ref, 0, given, near * cap, place, spread)
        return carry

    lax.fori_loop(0, tiles, one_tile, 0, unroll=math.gcd(tiles, 3))


def load_kernel(grad_hbm, pos_hbm, weight_hbm, count_hbm, own_hbm, grad_ref, pos_ref, weight_ref, count_ref, own_ref, info_ref, sems, *, near, cap):
    pairs = ((pos_hbm, pos_ref), (weight_hbm, weight_ref), (count_hbm, count_ref), (own_hbm, own_ref), (grad_hbm, grad_ref))
    copies = [pltpu.make_async_copy(source, target, sems.at[i]) for i, (source, target) in enumerate(pairs)]
    for copy in copies:
        copy.start()
    for copy in copies[:3]:
        copy.wait()
    slots, cells = pos_ref.shape
    last = pl.ds(cells - LANES, LANES)
    pos = pos_ref[:, last]
    local = pos - jnp.where(even_place(), 0, (near - 1) * cap)
    local = jnp.where((local >= 0) & (local < cap), local, -1)
    info_ref[0:slots, :] = local.astype(jnp.float32)
    info_ref[slots : 2 * slots, :] = merged_weights(pos, weight_ref[:, last], count_ref[:, last])
    for copy in copies[3:]:
        copy.wait()


def loaded(grad, pos, weight, count, own):
    near, cap = own.shape
    arrays = (grad, pos, weight, count, own)
    held = [jax.ShapeDtypeStruct(x.shape, x.dtype) for x in arrays]
    return pl.pallas_call(
        functools.partial(load_kernel, near=near, cap=cap),
        out_shape=(*held, jax.ShapeDtypeStruct((2 * pos.shape[0], LANES), jnp.float32)),
        in_specs=[HBM] * 5,
        out_specs=(VMEM,) * 6,
        scratch_shapes=[pltpu.SemaphoreType.DMA((5,))],
        compiler_params=pltpu.CompilerParams(vmem_limit_bytes=16 * MIB),
        cost_estimate=lasting(LOAD),
    )(*[in_hbm(x) for x in arrays])


def weights_kernel(pos_ref, weight_ref, count_ref, w_ref, *, first, near, cap):
    fill_tiles(pos_ref, weight_ref, count_ref, w_ref, first, w_ref.shape[1] // LANES, near, cap)


def dense_weights(pos, weight, count, near, cap, first, tiles, micros):
    return pl.pallas_call(
        functools.partial(weights_kernel, first=first, near=near, cap=cap),
        out_shape=jax.ShapeDtypeStruct((near * cap, tiles * LANES), jnp.bfloat16),
        in_specs=[VMEM] * 3,
        out_specs=VMEM,
        compiler_params=pltpu.CompilerParams(vmem_limit_bytes=16 * MIB),
        cost_estimate=lasting(micros),
    )(pos, weight, count)


def chosen(grad, wanted):
    hit = row_ids((grad.shape[1], wanted.shape[1])) == wanted
    onehot = jnp.where(hit, jnp.float32(1.0), jnp.float32(0.0)).astype(jnp.bfloat16)
    return jnp.dot(grad, onehot, preferred_element_type=jnp.float32).astype(jnp.bfloat16)


def outer_pick_kernel(grad_ref, asked_ref, out_ref):
    near = asked_ref.shape[0]
    wanted = jnp.where(even_place(), asked_ref[near - 1 : near, :], asked_ref[0:1, :])
    out_ref[...] = chosen(grad_ref[...], wanted)


def inner_pick_kernel(grad_ref, asked_ref, own_ref, out_ref, own_out):
    near = asked_ref.shape[0]
    wanted = jnp.where(even_place(), asked_ref[0:1, :], asked_ref[near - 1 : near, :])
    out_ref[...] = chosen(grad_ref[...], wanted)
    own_out[...] = chosen(grad_ref[...], own_ref[near // 2 : near // 2 + 1, :])


def picked(kernel, outputs, micros, grad, *asked):
    shape = jax.ShapeDtypeStruct((grad.shape[0], asked[0].shape[1]), grad.dtype)
    return pl.pallas_call(
        kernel,
        out_shape=(shape,) * outputs,
        in_specs=[VMEM] * (1 + len(asked)),
        out_specs=(VMEM,) * outputs,
        compiler_params=pltpu.CompilerParams(vmem_limit_bytes=16 * MIB),
        cost_estimate=lasting(micros),
    )(grad, *asked)


def half_rows(cols):
    return -(-cols // (2 * PACK)) * PACK


def pack_fold(total, edge_ref, sum_ref):
    cols, half = total.shape[0], edge_ref.shape[0]
    tail = cols // 8 * 8
    sum_ref[pl.ds(tail, 2 * half - tail), :] = jnp.zeros((2 * half - tail, LANES), jnp.float32)
    sum_ref[0:cols, :] = total
    upper = pltpu.roll(sum_ref[0:half, :], LANES // 2, 1)
    packed = jnp.where(lane_ids((half, LANES)) < LANES // 2, upper, sum_ref[half : 2 * half, :])
    edge_ref[...] = packed.astype(jnp.bfloat16)


def near_fold_kernel(pos_ref, weight_ref, count_ref, own_ref, inner_ref, w_ref, edge_ref, sum_ref, *, near, cap):
    fill_tiles(pos_ref, weight_ref, count_ref, w_ref, pos_ref.shape[1] // LANES - 1, 1, near, cap)
    total = jnp.dot(own_ref[...], w_ref[cap : 2 * cap, :], preferred_element_type=jnp.float32)
    total += jnp.dot(inner_ref[...], w_ref[2 * cap : 3 * cap, :], preferred_element_type=jnp.float32)
    pack_fold(total, edge_ref, sum_ref)


def near_fold(pos, weight, count, own, inner, near):
    cols, cap = own.shape
    half = half_rows(cols)
    return pl.pallas_call(
        functools.partial(near_fold_kernel, near=near, cap=cap),
        out_shape=(jax.ShapeDtypeStruct((near * cap, LANES), jnp.bfloat16), jax.ShapeDtypeStruct((half, LANES), jnp.bfloat16)),
        in_specs=[VMEM] * 5,
        out_specs=(VMEM,) * 2,
        scratch_shapes=[pltpu.VMEM((2 * half, LANES), jnp.float32)],
        compiler_params=pltpu.CompilerParams(vmem_limit_bytes=16 * MIB),
        cost_estimate=lasting(FOLD),
    )(pos, weight, count, own, inner)


def far_fold_kernel(info_ref, rows_ref, edge_ref, w_ref, sum_ref):
    slots, cap = info_ref.shape[0] // 2, rows_ref.shape[1]
    row = row_ids((PACK, LANES)).astype(jnp.int16)
    place = [x - row for x in spread_rows(info_ref[0:slots, :].astype(jnp.int32), jnp.int16)]
    fill_piece(w_ref, 0, pl.ds(0, LANES), cap, place, spread_rows(info_ref[slots:, :], jnp.bfloat16))
    pack_fold(jnp.dot(rows_ref[...], w_ref[...], preferred_element_type=jnp.float32), edge_ref, sum_ref)


def far_fold(info, rows):
    cols, cap = rows.shape
    half = half_rows(cols)
    return pl.pallas_call(
        far_fold_kernel,
        out_shape=jax.ShapeDtypeStruct((half, LANES), jnp.bfloat16),
        in_specs=[VMEM] * 2,
        out_specs=VMEM,
        scratch_shapes=[pltpu.VMEM((cap, LANES), jnp.bfloat16), pltpu.VMEM((2 * half, LANES), jnp.float32)],
        compiler_params=pltpu.CompilerParams(vmem_limit_bytes=16 * MIB),
        cost_estimate=lasting(FOLD),
    )(info, rows)


def mixed(parts, w_ref, lanes):
    cap = parts[0].shape[1]
    acc = None
    for i, part in enumerate(parts):
        term = jnp.dot(part[...], w_ref[pl.ds(i * cap, cap), lanes], preferred_element_type=jnp.float32)
        acc = term if acc is None else acc + term
    return acc


def unpack_fold(mirrors, src_ref, cols):
    fold = src_ref.shape[1]
    unused = jnp.full((1, LANES - fold), -1, jnp.int32)
    halves = []
    for shift in (0, LANES // 2):
        source = jnp.concatenate([unused, src_ref[...] + shift], axis=1)
        hit = row_ids((LANES, LANES)) == source
        onehot = jnp.where(hit, jnp.float32(1.0), jnp.float32(0.0)).astype(jnp.bfloat16)
        halves.append(sum(jnp.dot(m[...], onehot, preferred_element_type=jnp.float32) for m in mirrors))
    return jnp.concatenate(halves, axis=0)[0:cols]


def body_kernel(outer_ref, own_ref, inner_ref, early_ref, late_ref, last_ref, near_ref, far_ref, src_ref, out_hbm, buffer, sems, *, width):
    parts = (outer_ref, own_ref, inner_ref)
    copies, start = [], 0
    for w_ref in (early_ref, late_ref, last_ref):
        for inside in range(0, w_ref.shape[1], width):
            taken = min(width, w_ref.shape[1] - inside)
            total = mixed(parts, w_ref, pl.ds(inside, taken))
            if w_ref is last_ref:
                total += unpack_fold((near_ref, far_ref), src_ref, own_ref.shape[0])
            lanes = pl.ds(start, taken)
            buffer[:, lanes] = total.astype(jnp.bfloat16)
            copies.append(pltpu.make_async_copy(buffer.at[:, lanes], out_hbm.at[:, lanes], sems.at[len(copies)]))
            copies[-1].start()
            start += taken
    for copy in copies:
        copy.wait()


def body_sums(outer, own, inner, dense, mirrors, fold_src):
    cols, width = own.shape[0], 4 * LANES
    cells = sum(w.shape[1] for w in dense)
    steps = sum(-(-w.shape[1] // width) for w in dense)
    return pl.pallas_call(
        functools.partial(body_kernel, width=width),
        out_shape=jax.ShapeDtypeStruct((cols, cells), jnp.bfloat16),
        in_specs=[VMEM] * 9,
        out_specs=HBM,
        scratch_shapes=[pltpu.VMEM((cols, cells), jnp.bfloat16), pltpu.SemaphoreType.DMA((steps,))],
        compiler_params=pltpu.CompilerParams(vmem_limit_bytes=24 * MIB),
        cost_estimate=lasting(2.5),
    )(outer, own, inner, *dense, *mirrors, fold_src)


def local(analysis_grad, requests, slot_pos, slot_weight, slot_count, fold_src):
    near, cap = requests.shape
    tiles = slot_pos.shape[0] // LANES
    asked_inner = inner_swap(requests)
    asked_outer = outer_swap(requests)
    grad, pos, weight, count, own_asks, info = loaded(analysis_grad.T, slot_pos.T, slot_weight.T, slot_count[None, :], requests)
    info = outer_swap(info)
    for_inner, own = picked(inner_pick_kernel, 2, IPICK, grad, asked_inner, own_asks)
    early_w = dense_weights(pos, weight, count, near, cap, 0, EARLY_TILES, WA)
    asked_outer, for_inner, early_w = lax.optimization_barrier((asked_outer, for_inner, early_w))
    inner = inner_swap(for_inner)
    (for_outer,) = picked(outer_pick_kernel, 1, OPICK, grad, asked_outer)
    outer = outer_swap(for_outer)
    last_w, near_edge = near_fold(pos, weight, count, own, inner, near)
    near_mirror = half_away(near_edge)
    far_mirror = half_away_of_outer(far_fold(info, for_outer))
    late_w = dense_weights(pos, weight, count, near, cap, EARLY_TILES, tiles - EARLY_TILES - 1, FOLD)
    return body_sums(outer, own, inner, (early_w, late_w, last_w), (near_mirror, far_mirror), fold_src[None, :]).T


def solution(mesh):
    in_specs = (
        P(("members", "lon"), None),
        P("lon", None),
        P("lon", None),
        P("lon", None),
        P("lon"),
        P("lon"),
    )
    out_specs = P(("members", "lon"), None)
    return jax.shard_map(local, mesh=mesh, in_specs=in_specs, out_specs=out_specs, check_vma=False)
```

```python
import functools
import math

import jax
import jax.numpy as jnp
from jax import lax
from jax.experimental import pallas as pl
from jax.experimental.pallas import tpu as pltpu
from jax.sharding import PartitionSpec as P

LANES = 128
PACK = 16
MID_TILES = 12
MIB = 2**20
FLOPS_PER_MICRO = 10**9
OPICK = 3
IPICK = 0
LOAD = 0
MID = 30
REST = 1
EDGE = 1
BODY = 1
VMEM = pl.BlockSpec(memory_space=pltpu.VMEM)
HBM = pl.BlockSpec(memory_space=pltpu.HBM)
ANY = pl.BlockSpec(memory_space=pl.ANY)


def lasting(micros):
    return pl.CostEstimate(flops=int(micros * FLOPS_PER_MICRO), bytes_accessed=0, transcendentals=0)


def row_ids(shape):
    return lax.broadcasted_iota(jnp.int32, shape, 0)


def lane_ids(shape):
    return lax.broadcasted_iota(jnp.int32, shape, 1)


def sent(block, target):
    count = lax.axis_size("lon")
    return lax.ppermute(block, "lon", [(i, target(i, count)) for i in range(count)])


def inner_place(place, count):
    return place ^ 1


def outer_place(place, count):
    return (place - 1) % count if place % 2 == 0 else (place + 1) % count


def half_place(place, count):
    return (place + count // 2) % count


def is_even():
    return lax.rem(lax.axis_index("lon"), 2) == 0


def in_hbm(block):
    return pltpu.with_memory_space_constraint(block, pltpu.HBM)


def merged_weights(pos, weight, count):
    valid = row_ids(pos.shape) < count
    masked = jnp.where(valid, weight, jnp.float32(0.0))
    scale = masked / jnp.sum(masked, axis=0, keepdims=True)
    scale = scale.astype(jnp.bfloat16).astype(jnp.float32)
    merged = jnp.zeros(pos.shape, jnp.float32)
    for k in range(pos.shape[0]):
        merged += jnp.where(pos == pos[k : k + 1], scale[k : k + 1], jnp.float32(0.0))
    return merged


def spread_rows(rows, dtype):
    return [jnp.broadcast_to(rows[k : k + 1], (PACK, LANES)).astype(dtype) for k in range(rows.shape[0])]


def fill_piece(w_ref, first, lanes, count, place, spread):
    for group in range(count // PACK):
        acc = jnp.zeros((PACK, LANES), jnp.bfloat16)
        for k in range(len(place)):
            acc = jnp.where(place[k] == jnp.int16(group * PACK), spread[k], acc)
        w_ref[pl.ds(first + group * PACK, PACK), lanes] = acc


def fill_tiles(pos_ref, weight_ref, count_ref, w_ref, first, tiles, near, cap):
    even = is_even()
    row = row_ids((PACK, LANES)).astype(jnp.int16)

    def one_tile(tile, carry):
        taken = pl.ds(pl.multiple_of((first + tile) * LANES, LANES), LANES)
        given = pl.ds(pl.multiple_of(tile * LANES, LANES), LANES)
        pos = pos_ref[:, taken]
        spread = spread_rows(merged_weights(pos, weight_ref[:, taken], count_ref[:, taken]), jnp.bfloat16)
        turned = jnp.where(even, pos, pos + cap * (near - 1) - 2 * cap * lax.div(pos, cap))
        place = [x - row for x in spread_rows(turned, jnp.int16)]
        fill_piece(w_ref, 0, given, near * cap, place, spread)
        return carry

    lax.fori_loop(0, tiles, one_tile, 0, unroll=math.gcd(tiles, 3))


def load_kernel(*refs):
    count = (len(refs) - 1) // 2
    copies = [pltpu.make_async_copy(refs[i], refs[count + i], refs[-1].at[i]) for i in range(count)]
    for copy in copies:
        copy.start()
    for copy in copies:
        copy.wait()


def loaded(*arrays):
    return pl.pallas_call(
        load_kernel,
        out_shape=tuple(jax.ShapeDtypeStruct(x.shape, x.dtype) for x in arrays),
        in_specs=[HBM] * len(arrays),
        out_specs=(VMEM,) * len(arrays),
        scratch_shapes=[pltpu.SemaphoreType.DMA((len(arrays),))],
        compiler_params=pltpu.CompilerParams(vmem_limit_bytes=16 * MIB),
        cost_estimate=lasting(LOAD),
    )(*[in_hbm(x) for x in arrays])


def weights_kernel(after_ref, pos_ref, weight_ref, count_ref, w_ref, *, first, near, cap):
    del after_ref
    fill_tiles(pos_ref, weight_ref, count_ref, w_ref, first, w_ref.shape[1] // LANES, near, cap)


def dense_weights(after, pos, weight, count, near, cap, first, tiles, micros):
    return pl.pallas_call(
        functools.partial(weights_kernel, first=first, near=near, cap=cap),
        out_shape=jax.ShapeDtypeStruct((near * cap, tiles * LANES), jnp.bfloat16),
        in_specs=[ANY] + [VMEM] * 3,
        out_specs=VMEM,
        compiler_params=pltpu.CompilerParams(vmem_limit_bytes=16 * MIB),
        cost_estimate=lasting(micros),
    )(after, pos, weight, count)


def chosen(grad, wanted):
    hit = row_ids((grad.shape[1], wanted.shape[1])) == wanted
    onehot = jnp.where(hit, jnp.float32(1.0), jnp.float32(0.0)).astype(jnp.bfloat16)
    return jnp.dot(grad, onehot, preferred_element_type=jnp.float32).astype(jnp.bfloat16)


def outer_pick_kernel(grad_ref, asked_ref, out_ref):
    near = asked_ref.shape[0]
    wanted = jnp.where(is_even(), asked_ref[near - 1 : near, :], asked_ref[0:1, :])
    out_ref[...] = chosen(grad_ref[...], wanted)


def inner_pick_kernel(grad_ref, asked_ref, own_ref, after_ref, out_ref, own_out):
    del after_ref
    near = asked_ref.shape[0]
    wanted = jnp.where(is_even(), asked_ref[0:1, :], asked_ref[near - 1 : near, :])
    out_ref[...] = chosen(grad_ref[...], wanted)
    own_out[...] = chosen(grad_ref[...], own_ref[near // 2 : near // 2 + 1, :])


def picked(kernel, outputs, micros, grad, *asked):
    shape = jax.ShapeDtypeStruct((grad.shape[0], asked[0].shape[1]), grad.dtype)
    return pl.pallas_call(
        kernel,
        out_shape=(shape,) * outputs,
        in_specs=[VMEM] * min(len(asked) + 1, 3) + [ANY] * max(len(asked) - 2, 0),
        out_specs=(VMEM,) * outputs,
        compiler_params=pltpu.CompilerParams(vmem_limit_bytes=16 * MIB),
        cost_estimate=lasting(micros),
    )(grad, *asked)


def mixed(parts, w_ref, lanes):
    cap = parts[0].shape[1]
    acc = None
    for i, part in enumerate(parts):
        term = jnp.dot(part[...], w_ref[pl.ds(i * cap, cap), lanes], preferred_element_type=jnp.float32)
        acc = term if acc is None else acc + term
    return acc


def edge_kernel(outer_ref, own_ref, inner_ref, w_ref, sum_ref, edge_ref):
    cells, cols, half = w_ref.shape[1], own_ref.shape[0], edge_ref.shape[0]
    total = mixed((outer_ref, own_ref, inner_ref), w_ref, pl.ds(cells - LANES, LANES))
    tail = cols // 8 * 8
    sum_ref[pl.ds(tail, 2 * half - tail), :] = jnp.zeros((2 * half - tail, LANES), jnp.float32)
    sum_ref[0:cols, :] = total
    upper = pltpu.roll(sum_ref[0:half, :], LANES // 2, 1)
    packed = jnp.where(lane_ids((half, LANES)) < LANES // 2, upper, sum_ref[half : 2 * half, :])
    edge_ref[...] = packed.astype(jnp.bfloat16)


def edge_sums(outer, own, inner, dense):
    cols = own.shape[0]
    half = -(-cols // (2 * PACK)) * PACK
    return pl.pallas_call(
        edge_kernel,
        out_shape=(jax.ShapeDtypeStruct((2 * half, LANES), jnp.float32), jax.ShapeDtypeStruct((half, LANES), jnp.bfloat16)),
        in_specs=[VMEM] * 4,
        out_specs=(VMEM,) * 2,
        compiler_params=pltpu.CompilerParams(vmem_limit_bytes=16 * MIB),
        cost_estimate=lasting(EDGE),
    )(outer, own, inner, dense)


def body_kernel(outer_ref, own_ref, inner_ref, late_ref, early_ref, out_hbm, buffer, sems, *, steps):
    for i, (start, width) in enumerate(steps):
        ahead = late_ref.shape[1]
        w_ref, inside = (late_ref, start) if start < ahead else (early_ref, start - ahead)
        buffer[:, pl.ds(start, width)] = mixed((outer_ref, own_ref, inner_ref), w_ref, pl.ds(inside, width)).astype(jnp.bfloat16)
        pltpu.make_async_copy(buffer.at[:, pl.ds(start, width)], out_hbm.at[:, pl.ds(start, width)], sems.at[i]).start()
    for i, (start, width) in enumerate(steps):
        pltpu.make_async_copy(buffer.at[:, pl.ds(start, width)], out_hbm.at[:, pl.ds(start, width)], sems.at[i]).wait()


def cuts(first, last, width):
    return [(start, min(width, last - start)) for start in range(first, last, width)]


def body_sums(outer, own, inner, late_w, early_w):
    cols, ahead = own.shape[0], late_w.shape[1]
    cells = ahead + early_w.shape[1]
    steps = cuts(0, ahead, 4 * LANES) + cuts(ahead, cells - LANES, 4 * LANES)
    return pl.pallas_call(
        functools.partial(body_kernel, steps=steps),
        out_shape=jax.ShapeDtypeStruct((cols, cells), jnp.bfloat16),
        in_specs=[VMEM] * 5,
        out_specs=HBM,
        scratch_shapes=[pltpu.VMEM((cols, cells), jnp.bfloat16), pltpu.SemaphoreType.DMA((len(steps),))],
        compiler_params=pltpu.CompilerParams(vmem_limit_bytes=24 * MIB),
        cost_estimate=lasting(BODY),
    )(outer, own, inner, late_w, early_w)


def fold_kernel(whole_ref, sum_ref, mirror_ref, src_ref, out_ref):
    del whole_ref
    cols, half, fold = out_ref.shape[0], mirror_ref.shape[0], src_ref.shape[1]
    unused = jnp.full((1, LANES - fold), -1, jnp.int32)
    others = []
    for shift in (0, LANES // 2):
        source = jnp.concatenate([unused, src_ref[...] + shift], axis=1)
        hit = row_ids((LANES, LANES)) == source
        onehot = jnp.where(hit, jnp.float32(1.0), jnp.float32(0.0)).astype(jnp.bfloat16)
        others.append(jnp.dot(mirror_ref[...], onehot, preferred_element_type=jnp.float32))
    other = jnp.concatenate(others, axis=0)[0:cols]
    out_ref[...] = (sum_ref[0:cols, :] + other).astype(jnp.bfloat16)


def folded(whole, sums, mirror, fold_src):
    cols, cells = whole.shape
    last = cells // LANES - 1
    return pl.pallas_call(
        fold_kernel,
        grid=(1,),
        out_shape=jax.ShapeDtypeStruct((cols, cells), jnp.bfloat16),
        in_specs=[HBM, VMEM, VMEM, VMEM],
        out_specs=pl.BlockSpec((cols, LANES), lambda i: (0, last)),
        input_output_aliases={0: 0},
        compiler_params=pltpu.CompilerParams(vmem_limit_bytes=8 * MIB),
    )(whole, sums, mirror, fold_src)


def local(analysis_grad, requests, slot_pos, slot_weight, slot_count, fold_src):
    near, cap = requests.shape
    tiles = slot_pos.shape[0] // LANES
    rest = tiles - MID_TILES
    asked_inner = sent(requests, inner_place)
    asked_outer = sent(requests, outer_place)
    grad, pos, weight, count, own_asks = loaded(analysis_grad.T, slot_pos.T, slot_weight.T, slot_count[None, :], requests)
    (for_outer,) = picked(outer_pick_kernel, 1, OPICK, grad, asked_outer)
    outer = sent(for_outer, outer_place)
    for_inner, own = picked(inner_pick_kernel, 2, IPICK, grad, asked_inner, own_asks, for_outer)
    inner = sent(for_inner, inner_place)
    mid_w = dense_weights(for_inner, pos, weight, count, near, cap, rest, MID_TILES, MID)
    sums, edge = edge_sums(outer, own, inner, mid_w)
    mirror = sent(edge, half_place)
    rest_w = dense_weights(sums, pos, weight, count, near, cap, 0, rest, REST)
    whole = body_sums(outer, own, inner, rest_w, mid_w)
    return folded(whole, sums, mirror, fold_src[None, :]).T


def solution(mesh):
    in_specs = (
        P(("members", "lon"), None),
        P("lon", None),
        P("lon", None),
        P("lon", None),
        P("lon"),
        P("lon"),
    )
    out_specs = P(("members", "lon"), None)
    return jax.shard_map(local, mesh=mesh, in_specs=in_specs, out_specs=out_specs, check_vma=False)
```

```python
import functools

import jax
import jax.numpy as jnp
from jax import lax
from jax.experimental import pallas as pl
from jax.experimental.pallas import tpu as pltpu
from jax.sharding import PartitionSpec as P

LANES = 128
PACK = 16
MID_TILES = 10
MIB = 2**20
FLOPS_PER_MICRO = 10**9
OPICK = 3
IPICK = 0
LOAD = 0
MID = 30
EDGE = 1
BODY = 1
VMEM = pl.BlockSpec(memory_space=pltpu.VMEM)
HBM = pl.BlockSpec(memory_space=pltpu.HBM)
ANY = pl.BlockSpec(memory_space=pl.ANY)


def lasting(micros):
    return pl.CostEstimate(flops=int(micros * FLOPS_PER_MICRO), bytes_accessed=0, transcendentals=0)


def row_ids(shape):
    return lax.broadcasted_iota(jnp.int32, shape, 0)


def lane_ids(shape):
    return lax.broadcasted_iota(jnp.int32, shape, 1)


def sent(block, target):
    count = lax.axis_size("lon")
    return lax.ppermute(block, "lon", [(i, target(i, count)) for i in range(count)])


def inner_place(place, count):
    return place ^ 1


def outer_place(place, count):
    return (place - 1) % count if place % 2 == 0 else (place + 1) % count


def half_place(place, count):
    return (place + count // 2) % count


def is_even():
    return lax.rem(lax.axis_index("lon"), 2) == 0


def in_hbm(block):
    return pltpu.with_memory_space_constraint(block, pltpu.HBM)


def merged_weights(pos, weight, count):
    valid = row_ids(pos.shape) < count
    masked = jnp.where(valid, weight, jnp.float32(0.0))
    scale = masked / jnp.sum(masked, axis=0, keepdims=True)
    scale = scale.astype(jnp.bfloat16).astype(jnp.float32)
    merged = jnp.zeros(pos.shape, jnp.float32)
    for k in range(pos.shape[0]):
        merged += jnp.where(pos == pos[k : k + 1], scale[k : k + 1], jnp.float32(0.0))
    return merged


def spread_rows(rows, dtype):
    return [jnp.broadcast_to(rows[k : k + 1], (PACK, LANES)).astype(dtype) for k in range(rows.shape[0])]


def fill_piece(w_ref, first, lanes, count, place, spread):
    for group in range(count // PACK):
        acc = jnp.zeros((PACK, LANES), jnp.bfloat16)
        for k in range(len(place)):
            acc = jnp.where(place[k] == jnp.int16(group * PACK), spread[k], acc)
        w_ref[pl.ds(first + group * PACK, PACK), lanes] = acc


def fill_tile(pos_ref, weight_ref, count_ref, w_ref, source, target, near, cap):
    taken, given = pl.ds(source, LANES), pl.ds(target, LANES)
    row = row_ids((PACK, LANES)).astype(jnp.int16)
    pos = pos_ref[:, taken]
    spread = spread_rows(merged_weights(pos, weight_ref[:, taken], count_ref[:, taken]), jnp.bfloat16)
    turned = jnp.where(is_even(), pos, pos + cap * (near - 1) - 2 * cap * lax.div(pos, cap))
    place = [x - row for x in spread_rows(turned, jnp.int16)]
    fill_piece(w_ref, 0, given, near * cap, place, spread)


def fill_tiles(pos_ref, weight_ref, count_ref, w_ref, first, tiles, near, cap):
    def one_tile(tile, carry):
        source, target = pl.multiple_of((first + tile) * LANES, LANES), pl.multiple_of(tile * LANES, LANES)
        fill_tile(pos_ref, weight_ref, count_ref, w_ref, source, target, near, cap)
        return carry

    lax.fori_loop(0, tiles, one_tile, 0, unroll=2 - tiles % 2)


def load_kernel(*refs):
    count = (len(refs) - 1) // 2
    copies = [pltpu.make_async_copy(refs[i], refs[count + i], refs[-1].at[i]) for i in range(count)]
    for copy in copies:
        copy.start()
    for copy in copies:
        copy.wait()


def loaded(*arrays):
    return pl.pallas_call(
        load_kernel,
        out_shape=tuple(jax.ShapeDtypeStruct(x.shape, x.dtype) for x in arrays),
        in_specs=[HBM] * len(arrays),
        out_specs=(VMEM,) * len(arrays),
        scratch_shapes=[pltpu.SemaphoreType.DMA((len(arrays),))],
        compiler_params=pltpu.CompilerParams(vmem_limit_bytes=16 * MIB),
        cost_estimate=lasting(LOAD),
    )(*[in_hbm(x) for x in arrays])


def weights_kernel(after_ref, pos_ref, weight_ref, count_ref, w_ref, *, first, near, cap):
    del after_ref
    fill_tiles(pos_ref, weight_ref, count_ref, w_ref, first, w_ref.shape[1] // LANES, near, cap)


def dense_weights(after, pos, weight, count, near, cap, first, tiles, micros):
    return pl.pallas_call(
        functools.partial(weights_kernel, first=first, near=near, cap=cap),
        out_shape=jax.ShapeDtypeStruct((near * cap, tiles * LANES), jnp.bfloat16),
        in_specs=[ANY] + [VMEM] * 3,
        out_specs=VMEM,
        compiler_params=pltpu.CompilerParams(vmem_limit_bytes=16 * MIB),
        cost_estimate=lasting(micros),
    )(after, pos, weight, count)


def chosen(grad, wanted):
    hit = row_ids((grad.shape[1], wanted.shape[1])) == wanted
    onehot = jnp.where(hit, jnp.float32(1.0), jnp.float32(0.0)).astype(jnp.bfloat16)
    return jnp.dot(grad, onehot, preferred_element_type=jnp.float32).astype(jnp.bfloat16)


def outer_pick_kernel(grad_ref, asked_ref, out_ref):
    near = asked_ref.shape[0]
    wanted = jnp.where(is_even(), asked_ref[near - 1 : near, :], asked_ref[0:1, :])
    out_ref[...] = chosen(grad_ref[...], wanted)


def inner_pick_kernel(grad_ref, asked_ref, own_ref, after_ref, out_ref, own_out):
    del after_ref
    near = asked_ref.shape[0]
    wanted = jnp.where(is_even(), asked_ref[0:1, :], asked_ref[near - 1 : near, :])
    out_ref[...] = chosen(grad_ref[...], wanted)
    own_out[...] = chosen(grad_ref[...], own_ref[near // 2 : near // 2 + 1, :])


def picked(kernel, outputs, micros, grad, *asked):
    shape = jax.ShapeDtypeStruct((grad.shape[0], asked[0].shape[1]), grad.dtype)
    return pl.pallas_call(
        kernel,
        out_shape=(shape,) * outputs,
        in_specs=[VMEM] * min(len(asked) + 1, 3) + [ANY] * max(len(asked) - 2, 0),
        out_specs=(VMEM,) * outputs,
        compiler_params=pltpu.CompilerParams(vmem_limit_bytes=16 * MIB),
        cost_estimate=lasting(micros),
    )(grad, *asked)


def mixed(parts, w_ref, lanes):
    cap = parts[0].shape[1]
    acc = None
    for i, part in enumerate(parts):
        term = jnp.dot(part[...], w_ref[pl.ds(i * cap, cap), lanes], preferred_element_type=jnp.float32)
        acc = term if acc is None else acc + term
    return acc


def part_kernel(own_ref, inner_ref, w_ref, part_ref):
    cells, cap = w_ref.shape[1], own_ref.shape[1]
    last = pl.ds(cells - LANES, LANES)
    part = jnp.dot(own_ref[...], w_ref[cap : 2 * cap, last], preferred_element_type=jnp.float32)
    part_ref[...] = part + jnp.dot(inner_ref[...], w_ref[2 * cap : 3 * cap, last], preferred_element_type=jnp.float32)


def part_sums(own, inner, dense):
    return pl.pallas_call(
        part_kernel,
        out_shape=jax.ShapeDtypeStruct((own.shape[0], LANES), jnp.float32),
        in_specs=[VMEM] * 3,
        out_specs=VMEM,
        compiler_params=pltpu.CompilerParams(vmem_limit_bytes=16 * MIB),
        cost_estimate=lasting(EDGE),
    )(own, inner, dense)


def edge_kernel(outer_ref, part_ref, w_ref, sum_ref, edge_ref):
    cells, cols, half, cap = w_ref.shape[1], part_ref.shape[0], edge_ref.shape[0], outer_ref.shape[1]
    total = part_ref[...] + jnp.dot(outer_ref[...], w_ref[0:cap, pl.ds(cells - LANES, LANES)], preferred_element_type=jnp.float32)
    tail = cols // 8 * 8
    sum_ref[pl.ds(tail, 2 * half - tail), :] = jnp.zeros((2 * half - tail, LANES), jnp.float32)
    sum_ref[0:cols, :] = total
    upper = pltpu.roll(sum_ref[0:half, :], LANES // 2, 1)
    packed = jnp.where(lane_ids((half, LANES)) < LANES // 2, upper, sum_ref[half : 2 * half, :])
    edge_ref[...] = packed.astype(jnp.bfloat16)


def edge_sums(outer, part, dense):
    cols = part.shape[0]
    half = -(-cols // (2 * PACK)) * PACK
    return pl.pallas_call(
        edge_kernel,
        out_shape=(jax.ShapeDtypeStruct((2 * half, LANES), jnp.float32), jax.ShapeDtypeStruct((half, LANES), jnp.bfloat16)),
        in_specs=[VMEM] * 3,
        out_specs=(VMEM,) * 2,
        compiler_params=pltpu.CompilerParams(vmem_limit_bytes=16 * MIB),
        cost_estimate=lasting(EDGE),
    )(outer, part, dense)


def body_kernel(outer_ref, own_ref, inner_ref, pos_ref, weight_ref, count_ref, mid_ref, after_ref, out_hbm, buffer, rest_ref, sems, *, width):
    del after_ref
    parts = (outer_ref, own_ref, inner_ref)
    near, cap = len(parts), own_ref.shape[1]
    ahead, cells = rest_ref.shape[1], out_hbm.shape[1]
    spans = cuts(ahead, cells - LANES, width) + cuts(0, ahead, width)
    early = len(cuts(ahead, cells - LANES, width))
    tiles, copies = list(range(0, ahead, LANES)), []
    for i, (start, taken) in enumerate(spans):
        w_ref, inside = (rest_ref, start) if start < ahead else (mid_ref, start - ahead)
        lanes = pl.ds(start, taken)
        buffer[:, lanes] = mixed(parts, w_ref, pl.ds(inside, taken)).astype(jnp.bfloat16)
        copies.append(pltpu.make_async_copy(buffer.at[:, lanes], out_hbm.at[:, lanes], sems.at[i]))
        copies[-1].start()
        for tile in tiles[len(tiles) * i // early : len(tiles) * (i + 1) // early] if i < early else ():
            fill_tile(pos_ref, weight_ref, count_ref, rest_ref, tile, tile, near, cap)
    for copy in copies:
        copy.wait()


def cuts(first, last, width):
    return [(start, min(width, last - start)) for start in range(first, last, width)]


def body_sums(outer, own, inner, pos, weight, count, mid_w, after):
    cols, width = own.shape[0], 2 * LANES
    cells, kept = pos.shape[1], pos.shape[1] - mid_w.shape[1]
    steps = len(cuts(kept, cells - LANES, width)) + len(cuts(0, kept, width))
    return pl.pallas_call(
        functools.partial(body_kernel, width=width),
        out_shape=jax.ShapeDtypeStruct((cols, cells), jnp.bfloat16),
        in_specs=[VMEM] * 7 + [ANY],
        out_specs=HBM,
        scratch_shapes=[pltpu.VMEM((cols, cells), jnp.bfloat16), pltpu.VMEM((mid_w.shape[0], kept), jnp.bfloat16), pltpu.SemaphoreType.DMA((steps,))],
        compiler_params=pltpu.CompilerParams(vmem_limit_bytes=24 * MIB),
        cost_estimate=lasting(BODY),
    )(outer, own, inner, pos, weight, count, mid_w, after)


def fold_kernel(whole_ref, sum_ref, mirror_ref, src_ref, out_ref):
    del whole_ref
    cols, half, fold = out_ref.shape[0], mirror_ref.shape[0], src_ref.shape[1]
    unused = jnp.full((1, LANES - fold), -1, jnp.int32)
    sources = [jnp.concatenate([unused, src_ref[...] + shift], axis=1) for shift in (0, LANES // 2)]
    hit = row_ids((LANES, 2 * LANES)) == jnp.concatenate(sources, axis=1)
    onehot = jnp.where(hit, jnp.float32(1.0), jnp.float32(0.0)).astype(jnp.bfloat16)
    both = jnp.dot(mirror_ref[...], onehot, preferred_element_type=jnp.float32)
    other = jnp.concatenate([both[:, :LANES], both[:, LANES:]], axis=0)[0:cols]
    out_ref[...] = (sum_ref[0:cols, :] + other).astype(jnp.bfloat16)


def folded(whole, sums, mirror, fold_src):
    cols, cells = whole.shape
    last = cells // LANES - 1
    return pl.pallas_call(
        fold_kernel,
        grid=(1,),
        out_shape=jax.ShapeDtypeStruct((cols, cells), jnp.bfloat16),
        in_specs=[HBM, VMEM, VMEM, VMEM],
        out_specs=pl.BlockSpec((cols, LANES), lambda i: (0, last)),
        input_output_aliases={0: 0},
        compiler_params=pltpu.CompilerParams(vmem_limit_bytes=8 * MIB),
    )(whole, sums, mirror, fold_src)


def local(analysis_grad, requests, slot_pos, slot_weight, slot_count, fold_src):
    near, cap = requests.shape
    tiles = slot_pos.shape[0] // LANES
    rest = tiles - MID_TILES
    asked_inner = sent(requests, inner_place)
    asked_outer = sent(requests, outer_place)
    grad, pos, weight, count, own_asks = loaded(analysis_grad.T, slot_pos.T, slot_weight.T, slot_count[None, :], requests)
    (for_outer,) = picked(outer_pick_kernel, 1, OPICK, grad, asked_outer)
    outer = sent(for_outer, outer_place)
    for_inner, own = picked(inner_pick_kernel, 2, IPICK, grad, asked_inner, own_asks, for_outer)
    inner = sent(for_inner, inner_place)
    mid_w = dense_weights(for_inner, pos, weight, count, near, cap, rest, MID_TILES, MID)
    sums, edge = edge_sums(outer, part_sums(own, inner, mid_w), mid_w)
    mirror = sent(edge, half_place)
    whole = body_sums(outer, own, inner, pos, weight, count, mid_w, sums)
    return folded(whole, sums, mirror, fold_src[None, :]).T


def solution(mesh):
    in_specs = (
        P(("members", "lon"), None),
        P("lon", None),
        P("lon", None),
        P("lon", None),
        P("lon"),
        P("lon"),
    )
    out_specs = P(("members", "lon"), None)
    return jax.shard_map(local, mesh=mesh, in_specs=in_specs, out_specs=out_specs, check_vma=False)
```

```python
import functools

import jax
import jax.numpy as jnp
from jax import lax
from jax.experimental import pallas as pl
from jax.experimental.pallas import tpu as pltpu
from jax.sharding import PartitionSpec as P

LANES = 128
PACK = 16
MID_TILES = 10
MIB = 2**20
FLOPS_PER_MICRO = 10**9
OPICK = 3
IPICK = 0
LOAD = 0
MID = 30
EDGE = 1
BODY = 1
VMEM = pl.BlockSpec(memory_space=pltpu.VMEM)
HBM = pl.BlockSpec(memory_space=pltpu.HBM)
ANY = pl.BlockSpec(memory_space=pl.ANY)


def lasting(micros):
    return pl.CostEstimate(flops=int(micros * FLOPS_PER_MICRO), bytes_accessed=0, transcendentals=0)


def row_ids(shape):
    return lax.broadcasted_iota(jnp.int32, shape, 0)


def lane_ids(shape):
    return lax.broadcasted_iota(jnp.int32, shape, 1)


def sent(block, target):
    count = lax.axis_size("lon")
    return lax.ppermute(block, "lon", [(i, target(i, count)) for i in range(count)])


def inner_place(place, count):
    return place ^ 1


def outer_place(place, count):
    return (place - 1) % count if place % 2 == 0 else (place + 1) % count


def half_place(place, count):
    return (place + count // 2) % count


def is_even():
    return lax.rem(lax.axis_index("lon"), 2) == 0


def in_hbm(block):
    return pltpu.with_memory_space_constraint(block, pltpu.HBM)


def merged_weights(pos, weight, count):
    valid = row_ids(pos.shape) < count
    masked = jnp.where(valid, weight, jnp.float32(0.0))
    scale = masked / jnp.sum(masked, axis=0, keepdims=True)
    scale = scale.astype(jnp.bfloat16).astype(jnp.float32)
    merged = jnp.zeros(pos.shape, jnp.float32)
    for k in range(pos.shape[0]):
        merged += jnp.where(pos == pos[k : k + 1], scale[k : k + 1], jnp.float32(0.0))
    return merged


def spread_rows(rows, dtype):
    return [jnp.broadcast_to(rows[k : k + 1], (PACK, LANES)).astype(dtype) for k in range(rows.shape[0])]


def fill_piece(w_ref, first, lanes, count, place, spread):
    for group in range(count // PACK):
        acc = jnp.zeros((PACK, LANES), jnp.bfloat16)
        for k in range(len(place)):
            acc = jnp.where(place[k] == jnp.int16(group * PACK), spread[k], acc)
        w_ref[pl.ds(first + group * PACK, PACK), lanes] = acc


def fill_tile(pos_ref, weight_ref, count_ref, w_ref, source, target, near, cap):
    taken, given = pl.ds(source, LANES), pl.ds(target, LANES)
    row = row_ids((PACK, LANES)).astype(jnp.int16)
    pos = pos_ref[:, taken]
    spread = spread_rows(merged_weights(pos, weight_ref[:, taken], count_ref[:, taken]), jnp.bfloat16)
    turned = jnp.where(is_even(), pos, pos + cap * (near - 1) - 2 * cap * lax.div(pos, cap))
    place = [x - row for x in spread_rows(turned, jnp.int16)]
    fill_piece(w_ref, 0, given, near * cap, place, spread)


def fill_tiles(pos_ref, weight_ref, count_ref, w_ref, first, tiles, near, cap):
    def one_tile(tile, carry):
        source, target = pl.multiple_of((first + tile) * LANES, LANES), pl.multiple_of(tile * LANES, LANES)
        fill_tile(pos_ref, weight_ref, count_ref, w_ref, source, target, near, cap)
        return carry

    lax.fori_loop(0, tiles, one_tile, 0, unroll=2 - tiles % 2)


def load_kernel(*refs):
    count = (len(refs) - 1) // 2
    copies = [pltpu.make_async_copy(refs[i], refs[count + i], refs[-1].at[i]) for i in range(count)]
    for copy in copies:
        copy.start()
    for copy in copies:
        copy.wait()


def loaded(*arrays):
    return pl.pallas_call(
        load_kernel,
        out_shape=tuple(jax.ShapeDtypeStruct(x.shape, x.dtype) for x in arrays),
        in_specs=[HBM] * len(arrays),
        out_specs=(VMEM,) * len(arrays),
        scratch_shapes=[pltpu.SemaphoreType.DMA((len(arrays),))],
        compiler_params=pltpu.CompilerParams(vmem_limit_bytes=16 * MIB),
        cost_estimate=lasting(LOAD),
    )(*[in_hbm(x) for x in arrays])


def weights_kernel(after_ref, pos_ref, weight_ref, count_ref, w_ref, *, first, near, cap):
    del after_ref
    fill_tiles(pos_ref, weight_ref, count_ref, w_ref, first, w_ref.shape[1] // LANES, near, cap)


def dense_weights(after, pos, weight, count, near, cap, first, tiles, micros):
    return pl.pallas_call(
        functools.partial(weights_kernel, first=first, near=near, cap=cap),
        out_shape=jax.ShapeDtypeStruct((near * cap, tiles * LANES), jnp.bfloat16),
        in_specs=[ANY] + [VMEM] * 3,
        out_specs=VMEM,
        compiler_params=pltpu.CompilerParams(vmem_limit_bytes=16 * MIB),
        cost_estimate=lasting(micros),
    )(after, pos, weight, count)


def chosen(grad, wanted):
    hit = row_ids((grad.shape[1], wanted.shape[1])) == wanted
    onehot = jnp.where(hit, jnp.float32(1.0), jnp.float32(0.0)).astype(jnp.bfloat16)
    return jnp.dot(grad, onehot, preferred_element_type=jnp.float32).astype(jnp.bfloat16)


def outer_pick_kernel(grad_ref, asked_ref, out_ref):
    near = asked_ref.shape[0]
    wanted = jnp.where(is_even(), asked_ref[near - 1 : near, :], asked_ref[0:1, :])
    out_ref[...] = chosen(grad_ref[...], wanted)


def inner_pick_kernel(grad_ref, asked_ref, own_ref, after_ref, out_ref, own_out):
    del after_ref
    near = asked_ref.shape[0]
    wanted = jnp.where(is_even(), asked_ref[0:1, :], asked_ref[near - 1 : near, :])
    out_ref[...] = chosen(grad_ref[...], wanted)
    own_out[...] = chosen(grad_ref[...], own_ref[near // 2 : near // 2 + 1, :])


def picked(kernel, outputs, micros, grad, *asked):
    shape = jax.ShapeDtypeStruct((grad.shape[0], asked[0].shape[1]), grad.dtype)
    return pl.pallas_call(
        kernel,
        out_shape=(shape,) * outputs,
        in_specs=[VMEM] * min(len(asked) + 1, 3) + [ANY] * max(len(asked) - 2, 0),
        out_specs=(VMEM,) * outputs,
        compiler_params=pltpu.CompilerParams(vmem_limit_bytes=16 * MIB),
        cost_estimate=lasting(micros),
    )(grad, *asked)


def mixed(parts, w_ref, lanes):
    cap = parts[0].shape[1]
    acc = None
    for i, part in enumerate(parts):
        term = jnp.dot(part[...], w_ref[pl.ds(i * cap, cap), lanes], preferred_element_type=jnp.float32)
        acc = term if acc is None else acc + term
    return acc


def part_kernel(own_ref, inner_ref, w_ref, part_ref):
    cells, cap = w_ref.shape[1], own_ref.shape[1]
    last = pl.ds(cells - LANES, LANES)
    part = jnp.dot(own_ref[...], w_ref[cap : 2 * cap, last], preferred_element_type=jnp.float32)
    part_ref[...] = part + jnp.dot(inner_ref[...], w_ref[2 * cap : 3 * cap, last], preferred_element_type=jnp.float32)


def part_sums(own, inner, dense):
    return pl.pallas_call(
        part_kernel,
        out_shape=jax.ShapeDtypeStruct((own.shape[0], LANES), jnp.float32),
        in_specs=[VMEM] * 3,
        out_specs=VMEM,
        compiler_params=pltpu.CompilerParams(vmem_limit_bytes=16 * MIB),
        cost_estimate=lasting(EDGE),
    )(own, inner, dense)


def edge_kernel(outer_ref, part_ref, w_ref, sum_ref, edge_ref):
    cells, cols, half, cap = w_ref.shape[1], part_ref.shape[0], edge_ref.shape[0], outer_ref.shape[1]
    total = part_ref[...] + jnp.dot(outer_ref[...], w_ref[0:cap, pl.ds(cells - LANES, LANES)], preferred_element_type=jnp.float32)
    tail = cols // 8 * 8
    sum_ref[pl.ds(tail, 2 * half - tail), :] = jnp.zeros((2 * half - tail, LANES), jnp.float32)
    sum_ref[0:cols, :] = total
    upper = pltpu.roll(sum_ref[0:half, :], LANES // 2, 1)
    packed = jnp.where(lane_ids((half, LANES)) < LANES // 2, upper, sum_ref[half : 2 * half, :])
    edge_ref[...] = packed.astype(jnp.bfloat16)


def edge_sums(outer, part, dense):
    cols = part.shape[0]
    half = -(-cols // (2 * PACK)) * PACK
    return pl.pallas_call(
        edge_kernel,
        out_shape=(jax.ShapeDtypeStruct((2 * half, LANES), jnp.float32), jax.ShapeDtypeStruct((half, LANES), jnp.bfloat16)),
        in_specs=[VMEM] * 3,
        out_specs=(VMEM,) * 2,
        compiler_params=pltpu.CompilerParams(vmem_limit_bytes=16 * MIB),
        cost_estimate=lasting(EDGE),
    )(outer, part, dense)


def body_kernel(outer_ref, own_ref, inner_ref, pos_ref, weight_ref, count_ref, mid_ref, after_ref, out_hbm, buffer, rest_ref, sems, *, width):
    del after_ref
    parts = (outer_ref, own_ref, inner_ref)
    near, cap = len(parts), own_ref.shape[1]
    ahead, cells = rest_ref.shape[1], out_hbm.shape[1]
    spans = cuts(ahead, cells - LANES, width) + cuts(0, ahead, width)
    early = len(cuts(ahead, cells - LANES, width))
    tiles, copies = list(range(0, ahead, LANES)), []
    for i, (start, taken) in enumerate(spans):
        w_ref, inside = (rest_ref, start) if start < ahead else (mid_ref, start - ahead)
        lanes = pl.ds(start, taken)
        buffer[:, lanes] = mixed(parts, w_ref, pl.ds(inside, taken)).astype(jnp.bfloat16)
        copies.append(pltpu.make_async_copy(buffer.at[:, lanes], out_hbm.at[:, lanes], sems.at[i]))
        copies[-1].start()
        for tile in tiles[len(tiles) * i // early : len(tiles) * (i + 1) // early] if i < early else ():
            fill_tile(pos_ref, weight_ref, count_ref, rest_ref, tile, tile, near, cap)
    for copy in copies:
        copy.wait()


def cuts(first, last, width):
    return [(start, min(width, last - start)) for start in range(first, last, width)]


def body_sums(outer, own, inner, pos, weight, count, mid_w, after):
    cols, width = own.shape[0], 4 * LANES
    cells, kept = pos.shape[1], pos.shape[1] - mid_w.shape[1]
    steps = len(cuts(kept, cells - LANES, width)) + len(cuts(0, kept, width))
    return pl.pallas_call(
        functools.partial(body_kernel, width=width),
        out_shape=jax.ShapeDtypeStruct((cols, cells), jnp.bfloat16),
        in_specs=[VMEM] * 7 + [ANY],
        out_specs=HBM,
        scratch_shapes=[pltpu.VMEM((cols, cells), jnp.bfloat16), pltpu.VMEM((mid_w.shape[0], kept), jnp.bfloat16), pltpu.SemaphoreType.DMA((steps,))],
        compiler_params=pltpu.CompilerParams(vmem_limit_bytes=24 * MIB),
        cost_estimate=lasting(BODY),
    )(outer, own, inner, pos, weight, count, mid_w, after)


def fold_kernel(whole_ref, sum_ref, mirror_ref, src_ref, out_ref):
    del whole_ref
    cols, half, fold = out_ref.shape[0], mirror_ref.shape[0], src_ref.shape[1]
    unused = jnp.full((1, LANES - fold), -1, jnp.int32)
    sources = [jnp.concatenate([unused, src_ref[...] + shift], axis=1) for shift in (0, LANES // 2)]
    hit = row_ids((LANES, 2 * LANES)) == jnp.concatenate(sources, axis=1)
    onehot = jnp.where(hit, jnp.float32(1.0), jnp.float32(0.0)).astype(jnp.bfloat16)
    both = jnp.dot(mirror_ref[...], onehot, preferred_element_type=jnp.float32)
    other = jnp.concatenate([both[:, :LANES], both[:, LANES:]], axis=0)[0:cols]
    out_ref[...] = (sum_ref[0:cols, :] + other).astype(jnp.bfloat16)


def folded(whole, sums, mirror, fold_src):
    cols, cells = whole.shape
    last = cells // LANES - 1
    return pl.pallas_call(
        fold_kernel,
        grid=(1,),
        out_shape=jax.ShapeDtypeStruct((cols, cells), jnp.bfloat16),
        in_specs=[HBM, VMEM, VMEM, VMEM],
        out_specs=pl.BlockSpec((cols, LANES), lambda i: (0, last)),
        input_output_aliases={0: 0},
        compiler_params=pltpu.CompilerParams(vmem_limit_bytes=8 * MIB),
    )(whole, sums, mirror, fold_src)


def local(analysis_grad, requests, slot_pos, slot_weight, slot_count, fold_src):
    near, cap = requests.shape
    tiles = slot_pos.shape[0] // LANES
    rest = tiles - MID_TILES
    asked_inner = sent(requests, inner_place)
    asked_outer = sent(requests, outer_place)
    grad, pos, weight, count, own_asks = loaded(analysis_grad.T, slot_pos.T, slot_weight.T, slot_count[None, :], requests)
    (for_outer,) = picked(outer_pick_kernel, 1, OPICK, grad, asked_outer)
    outer = sent(for_outer, outer_place)
    for_inner, own = picked(inner_pick_kernel, 2, IPICK, grad, asked_inner, own_asks, for_outer)
    inner = sent(for_inner, inner_place)
    mid_w = dense_weights(for_inner, pos, weight, count, near, cap, rest, MID_TILES, MID)
    sums, edge = edge_sums(outer, part_sums(own, inner, mid_w), mid_w)
    mirror = sent(edge, half_place)
    whole = body_sums(outer, own, inner, pos, weight, count, mid_w, sums)
    return folded(whole, sums, mirror, fold_src[None, :]).T


def solution(mesh):
    in_specs = (
        P(("members", "lon"), None),
        P("lon", None),
        P("lon", None),
        P("lon", None),
        P("lon"),
        P("lon"),
    )
    out_specs = P(("members", "lon"), None)
    return jax.shard_map(local, mesh=mesh, in_specs=in_specs, out_specs=out_specs, check_vma=False)
```

```python
import functools

import jax
import jax.numpy as jnp
from jax import lax
from jax.experimental import pallas as pl
from jax.experimental.pallas import tpu as pltpu
from jax.sharding import PartitionSpec as P

LANES = 128
PACK = 16
MID_TILES = 10
MIB = 2**20
FLOPS_PER_MICRO = 10**9
OPICK = 3
IPICK = 0
LOAD = 0
MID = 30
EDGE = 1
BODY = 1
VMEM = pl.BlockSpec(memory_space=pltpu.VMEM)
HBM = pl.BlockSpec(memory_space=pltpu.HBM)
ANY = pl.BlockSpec(memory_space=pl.ANY)


def lasting(micros):
    return pl.CostEstimate(flops=int(micros * FLOPS_PER_MICRO), bytes_accessed=0, transcendentals=0)


def row_ids(shape):
    return lax.broadcasted_iota(jnp.int32, shape, 0)


def lane_ids(shape):
    return lax.broadcasted_iota(jnp.int32, shape, 1)


def sent(block, target):
    count = lax.axis_size("lon")
    return lax.ppermute(block, "lon", [(i, target(i, count)) for i in range(count)])


def inner_place(place, count):
    return place ^ 1


def outer_place(place, count):
    return (place - 1) % count if place % 2 == 0 else (place + 1) % count


def half_place(place, count):
    return (place + count // 2) % count


def is_even():
    return lax.rem(lax.axis_index("lon"), 2) == 0


def in_hbm(block):
    return pltpu.with_memory_space_constraint(block, pltpu.HBM)


def merged_weights(pos, weight, count):
    valid = row_ids(pos.shape) < count
    masked = jnp.where(valid, weight, jnp.float32(0.0))
    scale = masked / jnp.sum(masked, axis=0, keepdims=True)
    scale = scale.astype(jnp.bfloat16).astype(jnp.float32)
    merged = jnp.zeros(pos.shape, jnp.float32)
    for k in range(pos.shape[0]):
        merged += jnp.where(pos == pos[k : k + 1], scale[k : k + 1], jnp.float32(0.0))
    return merged


def spread_rows(rows, dtype):
    return [jnp.broadcast_to(rows[k : k + 1], (PACK, LANES)).astype(dtype) for k in range(rows.shape[0])]


def fill_piece(w_ref, first, lanes, count, place, spread):
    for group in range(count // PACK):
        acc = jnp.zeros((PACK, LANES), jnp.bfloat16)
        for k in range(len(place)):
            acc = jnp.where(place[k] == jnp.int16(group * PACK), spread[k], acc)
        w_ref[pl.ds(first + group * PACK, PACK), lanes] = acc


def fill_tile(pos_ref, weight_ref, count_ref, w_ref, source, target, near, cap):
    taken, given = pl.ds(source, LANES), pl.ds(target, LANES)
    row = row_ids((PACK, LANES)).astype(jnp.int16)
    pos = pos_ref[:, taken]
    spread = spread_rows(merged_weights(pos, weight_ref[:, taken], count_ref[:, taken]), jnp.bfloat16)
    turned = jnp.where(is_even(), pos, pos + cap * (near - 1) - 2 * cap * lax.div(pos, cap))
    place = [x - row for x in spread_rows(turned, jnp.int16)]
    fill_piece(w_ref, 0, given, near * cap, place, spread)


def fill_tiles(pos_ref, weight_ref, count_ref, w_ref, first, tiles, near, cap):
    def one_tile(tile, carry):
        source, target = pl.multiple_of((first + tile) * LANES, LANES), pl.multiple_of(tile * LANES, LANES)
        fill_tile(pos_ref, weight_ref, count_ref, w_ref, source, target, near, cap)
        return carry

    lax.fori_loop(0, tiles, one_tile, 0, unroll=2 - tiles % 2)


def load_kernel(*refs):
    count = (len(refs) - 1) // 2
    copies = [pltpu.make_async_copy(refs[i], refs[count + i], refs[-1].at[i]) for i in range(count)]
    for copy in copies:
        copy.start()
    for copy in copies:
        copy.wait()


def loaded(*arrays):
    return pl.pallas_call(
        load_kernel,
        out_shape=tuple(jax.ShapeDtypeStruct(x.shape, x.dtype) for x in arrays),
        in_specs=[HBM] * len(arrays),
        out_specs=(VMEM,) * len(arrays),
        scratch_shapes=[pltpu.SemaphoreType.DMA((len(arrays),))],
        compiler_params=pltpu.CompilerParams(vmem_limit_bytes=16 * MIB),
        cost_estimate=lasting(LOAD),
    )(*[in_hbm(x) for x in arrays])


def weights_kernel(after_ref, pos_ref, weight_ref, count_ref, w_ref, *, first, near, cap):
    del after_ref
    fill_tiles(pos_ref, weight_ref, count_ref, w_ref, first, w_ref.shape[1] // LANES, near, cap)


def dense_weights(after, pos, weight, count, near, cap, first, tiles, micros):
    return pl.pallas_call(
        functools.partial(weights_kernel, first=first, near=near, cap=cap),
        out_shape=jax.ShapeDtypeStruct((near * cap, tiles * LANES), jnp.bfloat16),
        in_specs=[ANY] + [VMEM] * 3,
        out_specs=VMEM,
        compiler_params=pltpu.CompilerParams(vmem_limit_bytes=16 * MIB),
        cost_estimate=lasting(micros),
    )(after, pos, weight, count)


def chosen(grad, wanted):
    hit = row_ids((grad.shape[1], wanted.shape[1])) == wanted
    onehot = jnp.where(hit, jnp.float32(1.0), jnp.float32(0.0)).astype(jnp.bfloat16)
    return jnp.dot(grad, onehot, preferred_element_type=jnp.float32).astype(jnp.bfloat16)


def outer_pick_kernel(grad_ref, asked_ref, out_ref):
    near = asked_ref.shape[0]
    wanted = jnp.where(is_even(), asked_ref[near - 1 : near, :], asked_ref[0:1, :])
    out_ref[...] = chosen(grad_ref[...], wanted)


def inner_pick_kernel(grad_ref, asked_ref, own_ref, after_ref, out_ref, own_out):
    del after_ref
    near = asked_ref.shape[0]
    wanted = jnp.where(is_even(), asked_ref[0:1, :], asked_ref[near - 1 : near, :])
    out_ref[...] = chosen(grad_ref[...], wanted)
    own_out[...] = chosen(grad_ref[...], own_ref[near // 2 : near // 2 + 1, :])


def picked(kernel, outputs, micros, grad, *asked):
    shape = jax.ShapeDtypeStruct((grad.shape[0], asked[0].shape[1]), grad.dtype)
    return pl.pallas_call(
        kernel,
        out_shape=(shape,) * outputs,
        in_specs=[VMEM] * min(len(asked) + 1, 3) + [ANY] * max(len(asked) - 2, 0),
        out_specs=(VMEM,) * outputs,
        compiler_params=pltpu.CompilerParams(vmem_limit_bytes=16 * MIB),
        cost_estimate=lasting(micros),
    )(grad, *asked)


def mixed(parts, w_ref, lanes):
    cap = parts[0].shape[1]
    acc = None
    for i, part in enumerate(parts):
        term = jnp.dot(part[...], w_ref[pl.ds(i * cap, cap), lanes], preferred_element_type=jnp.float32)
        acc = term if acc is None else acc + term
    return acc


def part_kernel(own_ref, inner_ref, w_ref, part_ref):
    cells, cap = w_ref.shape[1], own_ref.shape[1]
    last = pl.ds(cells - LANES, LANES)
    part = jnp.dot(own_ref[...], w_ref[cap : 2 * cap, last], preferred_element_type=jnp.float32)
    part_ref[...] = part + jnp.dot(inner_ref[...], w_ref[2 * cap : 3 * cap, last], preferred_element_type=jnp.float32)


def part_sums(own, inner, dense):
    return pl.pallas_call(
        part_kernel,
        out_shape=jax.ShapeDtypeStruct((own.shape[0], LANES), jnp.float32),
        in_specs=[VMEM] * 3,
        out_specs=VMEM,
        compiler_params=pltpu.CompilerParams(vmem_limit_bytes=16 * MIB),
        cost_estimate=lasting(EDGE),
    )(own, inner, dense)


def edge_kernel(outer_ref, part_ref, w_ref, sum_ref, edge_ref):
    cells, cols, half, cap = w_ref.shape[1], part_ref.shape[0], edge_ref.shape[0], outer_ref.shape[1]
    total = part_ref[...] + jnp.dot(outer_ref[...], w_ref[0:cap, pl.ds(cells - LANES, LANES)], preferred_element_type=jnp.float32)
    sum_ref[...] = total
    upper = pltpu.roll(total[0:half], LANES // 2, 1)
    lower = jnp.concatenate([total[half:cols], jnp.zeros((2 * half - cols, LANES), jnp.float32)], axis=0)
    packed = jnp.where(lane_ids((half, LANES)) < LANES // 2, upper, lower)
    edge_ref[...] = packed.astype(jnp.bfloat16)


def edge_sums(outer, part, dense):
    cols = part.shape[0]
    half = -(-cols // (2 * PACK)) * PACK
    return pl.pallas_call(
        edge_kernel,
        out_shape=(jax.ShapeDtypeStruct((cols, LANES), jnp.float32), jax.ShapeDtypeStruct((half, LANES), jnp.bfloat16)),
        in_specs=[VMEM] * 3,
        out_specs=(VMEM,) * 2,
        compiler_params=pltpu.CompilerParams(vmem_limit_bytes=16 * MIB),
        cost_estimate=lasting(EDGE),
    )(outer, part, dense)


def body_kernel(outer_ref, own_ref, inner_ref, pos_ref, weight_ref, count_ref, mid_ref, after_ref, out_hbm, buffer, rest_ref, sems, *, width):
    del after_ref
    parts = (outer_ref, own_ref, inner_ref)
    near, cap = len(parts), own_ref.shape[1]
    ahead, cells = rest_ref.shape[1], out_hbm.shape[1]
    spans = cuts(ahead, cells - LANES, width) + cuts(0, ahead, width)
    early = len(cuts(ahead, cells - LANES, width))
    tiles, copies = list(range(0, ahead, LANES)), []
    for i, (start, taken) in enumerate(spans):
        w_ref, inside = (rest_ref, start) if start < ahead else (mid_ref, start - ahead)
        lanes = pl.ds(start, taken)
        buffer[:, lanes] = mixed(parts, w_ref, pl.ds(inside, taken)).astype(jnp.bfloat16)
        copies.append(pltpu.make_async_copy(buffer.at[:, lanes], out_hbm.at[:, lanes], sems.at[i]))
        copies[-1].start()
        for tile in tiles[len(tiles) * i // early : len(tiles) * (i + 1) // early] if i < early else ():
            fill_tile(pos_ref, weight_ref, count_ref, rest_ref, tile, tile, near, cap)
    for copy in copies:
        copy.wait()


def cuts(first, last, width):
    return [(start, min(width, last - start)) for start in range(first, last, width)]


def body_sums(outer, own, inner, pos, weight, count, mid_w, after):
    cols, width = own.shape[0], 4 * LANES
    cells, kept = pos.shape[1], pos.shape[1] - mid_w.shape[1]
    steps = len(cuts(kept, cells - LANES, width)) + len(cuts(0, kept, width))
    return pl.pallas_call(
        functools.partial(body_kernel, width=width),
        out_shape=jax.ShapeDtypeStruct((cols, cells), jnp.bfloat16),
        in_specs=[VMEM] * 7 + [ANY],
        out_specs=HBM,
        scratch_shapes=[pltpu.VMEM((cols, cells), jnp.bfloat16), pltpu.VMEM((mid_w.shape[0], kept), jnp.bfloat16), pltpu.SemaphoreType.DMA((steps,))],
        compiler_params=pltpu.CompilerParams(vmem_limit_bytes=24 * MIB),
        cost_estimate=lasting(BODY),
    )(outer, own, inner, pos, weight, count, mid_w, after)


def fold_kernel(whole_ref, sum_ref, mirror_ref, src_ref, out_ref):
    del whole_ref
    cols, half, fold = out_ref.shape[0], mirror_ref.shape[0], src_ref.shape[1]
    unused = jnp.full((1, LANES - fold), -1, jnp.int32)
    sources = [jnp.concatenate([unused, src_ref[...] + shift], axis=1) for shift in (0, LANES // 2)]
    hit = row_ids((LANES, 2 * LANES)) == jnp.concatenate(sources, axis=1)
    onehot = jnp.where(hit, jnp.float32(1.0), jnp.float32(0.0)).astype(jnp.bfloat16)
    both = jnp.dot(mirror_ref[...], onehot, preferred_element_type=jnp.float32)
    other = jnp.concatenate([both[:, :LANES], both[:, LANES:]], axis=0)[0:cols]
    out_ref[...] = (sum_ref[...] + other).astype(jnp.bfloat16)


def folded(whole, sums, mirror, fold_src):
    cols, cells = whole.shape
    last = cells // LANES - 1
    return pl.pallas_call(
        fold_kernel,
        grid=(1,),
        out_shape=jax.ShapeDtypeStruct((cols, cells), jnp.bfloat16),
        in_specs=[HBM, VMEM, VMEM, VMEM],
        out_specs=pl.BlockSpec((cols, LANES), lambda i: (0, last)),
        input_output_aliases={0: 0},
        compiler_params=pltpu.CompilerParams(vmem_limit_bytes=8 * MIB),
    )(whole, sums, mirror, fold_src)


def local(analysis_grad, requests, slot_pos, slot_weight, slot_count, fold_src):
    near, cap = requests.shape
    tiles = slot_pos.shape[0] // LANES
    rest = tiles - MID_TILES
    asked_inner = sent(requests, inner_place)
    asked_outer = sent(requests, outer_place)
    grad, pos, weight, count, own_asks = loaded(analysis_grad.T, slot_pos.T, slot_weight.T, slot_count[None, :], requests)
    (for_outer,) = picked(outer_pick_kernel, 1, OPICK, grad, asked_outer)
    outer = sent(for_outer, outer_place)
    for_inner, own = picked(inner_pick_kernel, 2, IPICK, grad, asked_inner, own_asks, for_outer)
    inner = sent(for_inner, inner_place)
    mid_w = dense_weights(for_inner, pos, weight, count, near, cap, rest, MID_TILES, MID)
    sums, edge = edge_sums(outer, part_sums(own, inner, mid_w), mid_w)
    mirror = sent(edge, half_place)
    whole = body_sums(outer, own, inner, pos, weight, count, mid_w, sums)
    return folded(whole, sums, mirror, fold_src[None, :]).T


def solution(mesh):
    in_specs = (
        P(("members", "lon"), None),
        P("lon", None),
        P("lon", None),
        P("lon", None),
        P("lon"),
        P("lon"),
    )
    out_specs = P(("members", "lon"), None)
    return jax.shard_map(local, mesh=mesh, in_specs=in_specs, out_specs=out_specs, check_vma=False)
```
